32 devices in a mesh: section: 4 (over x, core), fsdp: 4 (over z), dp: 2 (over y).
Axes of the slice: x: 2, y: 2, z: 4, core: 2. Of those that a mesh axis runs over, the one named last changes fastest.
Arguments:
- section_inputs: bfloat16 [4, 2, 512, 4096], P('section', 'dp', 'fsdp'), may hold values from -6 to 6
- queries: bfloat16 [4, 2, 512, 4096], P('section', 'dp', 'fsdp'), may hold values from -110 to 110
- keys: bfloat16 [4, 2, 512, 1024], P('section', 'dp', 'fsdp'), may hold values from -4.5 to 4.5
- w_value: bfloat16 [4, 4096, 1024], P('section', 'fsdp'), may hold values from -0.09375 to 0.09375
- gain: bfloat16 [4, 4096], P('section', 'fsdp'), may hold values from 0.5 to 1.5
- section_grads_in: bfloat16 [4, 2, 512, 4096], P('section', 'dp', 'fsdp'), may hold values from -6 to 6
Outputs:
- passed_grads: bfloat16 [4, 2, 512, 4096], P('section', 'dp', 'fsdp')
- w_value_grad: bfloat16 [4, 4096, 1024], P('section', ('fsdp', 'dp'))
- gain_grad: float32 [4, 4096], P('section', ('fsdp', 'dp'))
The draws below stay inside these ranges and needn't reach their ends.
All inputs are finite; a program needn't handle non-finite values.
Results may differ from the reference program's by a relative error of at most 0.029.
Values may be sent and summed in bfloat16 or wider, within the bound.
No kernel may reach another device: no remote copies, remote signals or barrier semaphores. Data moves between devices by JAX's collectives and lax.ppermute only.
A program may use at most 64 MiB of HBM per device.

```python
import jax
import jax.numpy as jnp
from jax import lax

D = 4096
QH = 32
KVH = 8
DH = 128
MEM = 128
TOK_DEV = 128
GROUP = 4
KV = 1024
TOKENS = 512
SECTIONS = 4
DOCS = 2
N_FSDP = 4


def paired_draw(key):
    base = jax.random.fold_in(key, 101)
    key_draw = jax.random.fold_in(base, 1)
    query_draw = jax.random.fold_in(base, 2)
    key_rows = jnp.clip(jax.random.normal(key_draw, (SECTIONS, DOCS, TOKENS, KVH * DH), jnp.float32), -4.0, 4.0)
    query_rows = jnp.clip(jax.random.normal(query_draw, (SECTIONS, DOCS, TOKENS, QH * DH), jnp.float32), -4.0, 4.0)
    return (key_rows, query_rows)


def draw_queries(key, part):
    return paired_draw(key)[1].astype(jnp.bfloat16)


def draw_keys(key, part):
    return paired_draw(key)[0].astype(jnp.bfloat16)


def strengthened(drawn, stream_key, source, target, shards_of, factor):
    def block_of(axis_at):
        return (jnp.arange(drawn.shape[axis_at]) // (drawn.shape[axis_at] // shards_of)).reshape((-1,) + (1,) * (drawn.ndim - 1 - axis_at))

    near = jax.random.permutation(stream_key, shards_of)[block_of(target)]
    other_side = (block_of(target) + shards_of // 2) % shards_of
    return jnp.where((block_of(source) == near) | (block_of(source) == other_side), factor * drawn, drawn)


def block_scale(key, shape, shards, smallest, high):
    def one(position, shards_of):
        heights = jax.random.uniform(jax.random.fold_in(jax.random.fold_in(key, 6), position), (shards_of,), jnp.float32, smallest / len(shards), high / len(shards))
        return jnp.repeat(jnp.exp(heights), shape[position] // shards_of).reshape((-1,) + (1,) * (len(shape) - position - 1))

    factor_of = one(*shards[0])
    for cut in shards[1:]:
        factor_of = factor_of * one(*cut)
    return factor_of


def gaussian(key, dims, scale, reach, pieces=(), kind=jnp.bfloat16):
    values = jax.random.normal(key, dims, jnp.float32) * scale
    if len(pieces) > 0:
        values = block_scale(key, dims, pieces, -0.22, 0.18) * values
    return jnp.clip(values, min=-reach, max=reach).astype(kind)


def noise_with(rng, dims, deviation, reach, pieces, heavy, kind=jnp.bfloat16):
    values = deviation * jax.random.normal(rng, dims, jnp.float32)
    if pieces:
        values = values * block_scale(rng, dims, pieces, -0.22, 0.18)
    return jnp.clip(strengthened(values, jax.random.fold_in(rng, 3), *heavy), -reach, reach).astype(kind)


def setup_inputs(seed: int = 0) -> dict:
    key_list = jax.random.split(jax.random.key(seed), 7)
    section_inputs = noise_with(key_list[0], (SECTIONS, DOCS, TOKENS, D), 1.0, 6.0, ((0, 4), (1, 2), (2, 4)), (2, 3, 4, 2.0))
    queries = draw_queries(jax.random.fold_in(key_list[6], 71), 0)
    keys = draw_keys(jax.random.fold_in(key_list[6], 71), 0)
    w_value = gaussian(key_list[3], (SECTIONS, D, KV), D ** -0.5, 0.09375, ((0, 4), (1, 4)))
    gain = jnp.clip(1.0 + 0.1 * jax.random.normal(key_list[4], (SECTIONS, D), jnp.float32), 0.5, 1.5).astype(jnp.bfloat16)
    section_grads_in = gaussian(key_list[5], (SECTIONS, DOCS, TOKENS, D), 1.0, 6.0, ((0, 4), (1, 2), (2, 4)))
    return dict(section_inputs=section_inputs, queries=queries, keys=keys, w_value=w_value, gain=gain, section_grads_in=section_grads_in)


NEG_FILL = -1e+30
EPSILON = 1e-05

def section_backward(inputs, queries, keys, weight, gain, cotangent):
    wide = inputs.astype(jnp.float32)
    inv_rms = lax.rsqrt(lax.optimization_barrier(jnp.mean(wide * wide, axis=1, keepdims=True)) + EPSILON)
    normed = wide * inv_rms
    gain_float = gain.astype(jnp.float32)
    normed_b = (normed * gain_float).astype(jnp.bfloat16)
    positions = jnp.arange(TOKENS, dtype=jnp.int32)
    visible = (positions[None, :] <= positions[:, None]) | (positions[None, :] < MEM)
    query_groups = queries.reshape(TOKENS, KVH, GROUP, DH).transpose(1, 2, 0, 3)
    key_groups = keys.reshape(TOKENS, KVH, DH).transpose(1, 0, 2)
    grad_groups = cotangent.reshape(N_FSDP, TOK_DEV, KVH, GROUP, DH).transpose(2, 0, 1, 3, 4)

    def group_values(operands):
        query_group, key_group, grad_group = operands
        scores = jnp.einsum('htd,kd->htk', query_group.astype(jnp.float32), key_group.astype(jnp.float32)) * DH ** (-0.5)
        scores = jnp.where(visible[None], scores, NEG_FILL)
        rounded_probs = lax.optimization_barrier(jax.nn.softmax(scores, axis=2).astype(jnp.bfloat16))
        blocks = rounded_probs.astype(jnp.float32).reshape(GROUP, N_FSDP, TOK_DEV, TOKENS)
        partial_value = jnp.einsum('hftk,fthd->fkd', blocks, grad_group.astype(jnp.float32))
        rounded = lax.optimization_barrier(partial_value.astype(jnp.bfloat16))
        return lax.optimization_barrier(jnp.sum(rounded.astype(jnp.float32), axis=0))
    value_grad = lax.map(group_values, (query_groups, key_groups, grad_groups))
    value_grad = value_grad.transpose(1, 0, 2).reshape(TOKENS, KVH * DH).astype(jnp.bfloat16)
    normed_grad = jnp.dot(value_grad, weight.T, preferred_element_type=jnp.float32)
    scaled = normed_grad * gain_float
    inner_mean = lax.optimization_barrier(jnp.mean(scaled * normed, axis=1, keepdims=True))
    input_grad = (cotangent.astype(jnp.float32) + inv_rms * (scaled - normed * inner_mean)).astype(jnp.bfloat16)
    gain_terms = lax.optimization_barrier(jnp.sum((normed_grad * normed).reshape(N_FSDP, TOK_DEV, D), axis=1))
    gain_terms = lax.optimization_barrier(gain_terms.astype(jnp.bfloat16)).astype(jnp.float32)
    weight_terms = jnp.einsum('ftd,ftk->fdk', normed_b.reshape(N_FSDP, TOK_DEV, D).astype(jnp.float32), value_grad.reshape(N_FSDP, TOK_DEV, KVH * DH).astype(jnp.float32))
    weight_terms = lax.optimization_barrier(weight_terms.astype(jnp.bfloat16)).astype(jnp.float32)
    return (input_grad, lax.optimization_barrier(jnp.sum(weight_terms, axis=0)), lax.optimization_barrier(jnp.sum(gain_terms, axis=0)))

def reference(section_inputs, queries, keys, w_value, gain, section_grads_in):
    input_list = []
    weight_list = []
    gain_list = []
    for section_index in range(SECTIONS):
        weight_sum = jnp.zeros((D, KVH * DH), jnp.float32)
        gain_sum = jnp.zeros((D,), jnp.float32)
        produced = []
        for doc_index in range(DOCS):
            input_grad, weight_terms, gain_terms = section_backward(section_inputs[section_index, doc_index], queries[section_index, doc_index], keys[section_index, doc_index], w_value[section_index], gain[section_index], section_grads_in[section_index, doc_index])
            produced.append(input_grad)
            weight_sum = weight_sum + weight_terms
            gain_sum = gain_sum + gain_terms
        input_list.append(jnp.stack(produced))
        weight_list.append(weight_sum.astype(jnp.bfloat16))
        gain_list.append(gain_sum)
    input_stack = jnp.stack(input_list)
    passed = jnp.concatenate([input_stack[1:], input_stack[:1]], axis=0)
    return (passed, jnp.stack(weight_list), jnp.stack(gain_list))
```

```python
import functools

import jax
import jax.numpy as jnp
from jax import lax
from jax.experimental import pallas as pl
from jax.experimental.pallas import tpu as pltpu
from jax.sharding import PartitionSpec as P

DH = 128
MEM = 128
NEG_FILL = -1e30
EPSILON = 1e-05
LOG2E = 1.4426950408889634
VMEM_BYTES = 40 * 1024 * 1024

WHOLE = pl.BlockSpec(memory_space=pltpu.VMEM)
SCALAR = pl.BlockSpec(memory_space=pltpu.SMEM)
PARAMS = pltpu.CompilerParams(vmem_limit_bytes=VMEM_BYTES)


def shifted(block, axis, distance, wrap):
    count = lax.axis_size(axis)
    route = [
        (i, (i + distance) % count) for i in range(count) if wrap or 0 <= i + distance < count
    ]
    return lax.ppermute(block, axis, route)


def to_column_owner(block, distance):
    sections, count = lax.axis_size("section"), lax.axis_size("fsdp")
    route = [
        (s * count + f, ((s - 1) % sections) * count + (f - distance) % count)
        for s in range(sections)
        for f in range(count)
    ]
    return lax.ppermute(block, ("section", "fsdp"), route)


def attention_kernel(count, group, slot_ref, query_ref, grad_ref, *refs):
    key_refs, out_refs = refs[:count], refs[count:]
    rows = query_ref.shape[0]
    slot = slot_ref[0]
    heads = [slice(h * DH, (h + 1) * DH) for h in range(group)]
    query = jnp.concatenate([query_ref[:, h] for h in heads], axis=0)
    grad = jnp.concatenate([grad_ref[:, h] for h in heads], axis=0)
    keys = jnp.concatenate([ref[...] for ref in key_refs], axis=0)
    scores = lax.dot_general(
        keys, query, (((1,), (1,)), ((), ())), preferred_element_type=jnp.float32
    )
    key_at = lax.broadcasted_iota(jnp.int32, (rows, rows), 0)
    query_at = lax.broadcasted_iota(jnp.int32, (rows, rows), 1)
    visible = (key_at <= query_at) | (slot * rows + key_at < MEM)
    visible = jnp.concatenate([visible] * group, axis=1)
    parts = [jnp.where(visible, scores[:rows], NEG_FILL)]
    parts += [scores[d * rows : (d + 1) * rows] for d in range(1, count)]
    hidden = [jnp.where(slot >= d, 0.0, NEG_FILL) for d in range(count)]
    tops = [jnp.max(part, axis=0, keepdims=True) + hide for part, hide in zip(parts, hidden)]
    top = functools.reduce(jnp.maximum, tops)
    scale = DH ** (-0.5) * LOG2E
    weights = [
        jnp.exp2((part - (top - hide)) * scale) for part, hide in zip(parts, hidden)
    ]
    total = functools.reduce(
        jnp.add, [jnp.sum(weight, axis=0, keepdims=True) for weight in weights]
    )
    inverse = 1.0 / total
    probs = jnp.concatenate([(w * inverse).astype(jnp.bfloat16) for w in weights], axis=0)
    values = jnp.dot(probs, grad, preferred_element_type=jnp.float32)
    for d in range(count):
        out_refs[d][...] = values[d * rows : (d + 1) * rows].astype(jnp.bfloat16)


def attention(slot, queries, grads, key_blocks):
    rows, width = queries.shape
    kv_width = key_blocks[0].shape[1]
    group = width // kv_width
    count = len(key_blocks)
    wide = pl.BlockSpec((rows, group * DH), lambda g: (0, g))
    narrow = pl.BlockSpec((rows, DH), lambda g: (0, g))
    return pl.pallas_call(
        functools.partial(attention_kernel, count, group),
        grid=(kv_width // DH,),
        in_specs=[SCALAR, wide, wide] + [narrow] * count,
        out_specs=[narrow] * count,
        out_shape=[jax.ShapeDtypeStruct((rows, kv_width), jnp.bfloat16)] * count,
        compiler_params=PARAMS,
    )(slot, queries, grads, *key_blocks)


def normalise_kernel(count, slot_ref, x_ref, *out_refs):
    slot = slot_ref[0]
    x = x_ref[...].astype(jnp.float32)
    inv_rms = lax.rsqrt(jnp.mean(x * x, axis=1, keepdims=True) + EPSILON)
    width = x.shape[1] // count
    for d in range(count):
        start = pl.multiple_of(lax.rem(slot + d, count) * width, width)
        block = x_ref[:, pl.ds(start, width)].astype(jnp.float32)
        out_refs[d][...] = (block * inv_rms).astype(jnp.bfloat16)


def normalised_blocks(slot, x, count):
    rows, width = x.shape
    return pl.pallas_call(
        functools.partial(normalise_kernel, count),
        in_specs=[SCALAR, WHOLE],
        out_specs=[WHOLE] * count,
        out_shape=[jax.ShapeDtypeStruct((rows, width // count), jnp.bfloat16)] * count,
        compiler_params=PARAMS,
    )(slot, x)


def feature_kernel(count, weight_ref, gain_ref, *refs):
    value_refs, xhat_refs = refs[:count], refs[count : 2 * count]
    scaled_refs, gain_grad_ref = refs[2 * count : 3 * count], refs[3 * count]
    rows = value_refs[0].shape[0]
    values = jnp.concatenate([ref[...] for ref in value_refs], axis=0)
    normed_grad = lax.dot_general(
        values, weight_ref[...], (((1,), (1,)), ((), ())), preferred_element_type=jnp.float32
    )
    gain = gain_ref[...].astype(jnp.float32)
    gain_sum = jnp.zeros_like(gain)
    for d in range(count):
        part = normed_grad[d * rows : (d + 1) * rows]
        scaled_refs[d][...] = (part * gain).astype(jnp.bfloat16)
        gain_sum += jnp.sum(part * xhat_refs[d][...].astype(jnp.float32), axis=0, keepdims=True)
    gain_grad_ref[...] = gain_sum


def feature_grads(weight, gain, values, xhats):
    count = len(values)
    rows, kv_width = values[0].shape
    width = weight.shape[0]
    step = min(width, 256)
    whole = pl.BlockSpec((rows, kv_width), lambda c: (0, 0))
    column = pl.BlockSpec((rows, step), lambda c: (0, c))
    line = pl.BlockSpec((1, step), lambda c: (0, c))
    out = pl.pallas_call(
        functools.partial(feature_kernel, count),
        grid=(width // step,),
        in_specs=[pl.BlockSpec((step, kv_width), lambda c: (c, 0)), line]
        + [whole] * count
        + [column] * count,
        out_specs=[column] * count + [line],
        out_shape=[jax.ShapeDtypeStruct((rows, width), jnp.bfloat16)] * count
        + [jax.ShapeDtypeStruct((1, width), jnp.float32)],
        compiler_params=PARAMS,
    )(weight, gain, *values, *xhats)
    return out[:count], out[count]


def weight_kernel(count, half_ref, gain_ref, *refs):
    value_refs, xhat_refs, out_ref = refs[:count], refs[count : 2 * count], refs[2 * count]
    gain = gain_ref[...].astype(jnp.float32)
    normed = jnp.concatenate(
        [(ref[...].astype(jnp.float32) * gain).astype(jnp.bfloat16) for ref in xhat_refs], axis=0
    )
    values = jnp.concatenate([ref[...] for ref in value_refs], axis=0)
    out_ref[...] = lax.dot_general(
        normed, values, (((0,), (0,)), ((), ())), preferred_element_type=jnp.float32
    ).astype(out_ref.dtype)


def weight_grad(half, halves, gain, values, xhats, dtype):
    count = len(values)
    rows, kv_width = values[0].shape
    width = gain.shape[1] // halves
    step = min(width, 256)
    steps = width // step
    whole = pl.BlockSpec((rows, kv_width), lambda c, half_ref: (0, 0))
    column = pl.BlockSpec((rows, step), lambda c, half_ref: (0, half_ref[0] * steps + c))
    line = pl.BlockSpec((1, step), lambda c, half_ref: (0, half_ref[0] * steps + c))
    return pl.pallas_call(
        functools.partial(weight_kernel, count),
        grid_spec=pltpu.PrefetchScalarGridSpec(
            num_scalar_prefetch=1,
            grid=(steps,),
            in_specs=[line] + [whole] * count + [column] * count,
            out_specs=pl.BlockSpec((step, kv_width), lambda c, half_ref: (c, 0)),
        ),
        out_shape=jax.ShapeDtypeStruct((width, kv_width), dtype),
        compiler_params=PARAMS,
    )(half, gain, *values, *xhats)


def input_kernel(count, slot_ref, x_ref, grad_ref, *refs):
    scaled_refs, out_ref = refs[:count], refs[count]
    slot = slot_ref[0]
    x = x_ref[...].astype(jnp.float32)
    inv_rms = lax.rsqrt(jnp.mean(x * x, axis=1, keepdims=True) + EPSILON)
    width = x.shape[1] // count
    starts = [pl.multiple_of(lax.rem(slot + d, count) * width, width) for d in range(count)]
    inner = jnp.zeros_like(inv_rms)
    for d in range(count):
        xhat = x_ref[:, pl.ds(starts[d], width)].astype(jnp.float32) * inv_rms
        inner += jnp.sum(scaled_refs[d][...].astype(jnp.float32) * xhat, axis=1, keepdims=True)
    inner = inner / x.shape[1]
    for d in range(count):
        columns = pl.ds(starts[d], width)
        xhat = x_ref[:, columns].astype(jnp.float32) * inv_rms
        scaled = scaled_refs[d][...].astype(jnp.float32)
        grad = grad_ref[:, columns].astype(jnp.float32)
        out_ref[:, columns] = (grad + inv_rms * (scaled - xhat * inner)).astype(jnp.bfloat16)


def input_grad(slot, x, grads, scaled):
    count = len(scaled)
    return pl.pallas_call(
        functools.partial(input_kernel, count),
        in_specs=[SCALAR] + [WHOLE] * (2 + count),
        out_specs=WHOLE,
        out_shape=jax.ShapeDtypeStruct(x.shape, jnp.bfloat16),
        compiler_params=PARAMS,
    )(slot, x, grads, *scaled)


def per_device(section_inputs, queries, keys, w_value, gain, section_grads_in):
    count = lax.axis_size("fsdp")
    docs = lax.axis_size("dp")
    slot = lax.axis_index("fsdp").astype(jnp.int32)[None]
    half = lax.axis_index("dp").astype(jnp.int32)[None]
    x, cotangent, own_keys = section_inputs[0, 0], section_grads_in[0, 0], keys[0, 0]
    assert MEM <= x.shape[0] and docs == 2

    key_blocks = [own_keys] + [shifted(own_keys, "fsdp", d, False) for d in range(1, count)]
    xhat_out = normalised_blocks(slot, x, count)
    xhats = [xhat_out[0]] + [shifted(xhat_out[d], "fsdp", d, True) for d in range(1, count)]
    next_x = shifted(x, "section", -1, True)
    next_grad = shifted(cotangent, "section", -1, True)

    terms = attention(slot, queries[0, 0], cotangent, key_blocks)
    arrived = [terms[0]] + [shifted(terms[d], "fsdp", -d, False) for d in range(1, count)]
    value = sum(t.astype(jnp.float32) for t in arrived).astype(jnp.bfloat16)
    values = [value] + [shifted(value, "fsdp", d, True) for d in range(1, count)]

    scaled, gain_sum = feature_grads(w_value[0], gain, values, xhats)
    returned = [to_column_owner(scaled[d], d) for d in range(count)]

    sent_weight = weight_grad(1 - half, docs, gain, values, xhats, jnp.bfloat16)
    got_weight = shifted(sent_weight, "dp", 1, True)
    gain_halves = gain_sum.reshape(docs, -1)
    got_gain = shifted(
        lax.dynamic_index_in_dim(gain_halves, 1 - half[0], 0, keepdims=True), "dp", 1, True
    )
    own_weight = weight_grad(half, docs, gain, values, xhats, jnp.float32)
    weight_out = (own_weight + got_weight.astype(jnp.float32)).astype(jnp.bfloat16)
    gain_out = lax.dynamic_index_in_dim(gain_halves, half[0], 0, keepdims=True) + got_gain

    passed = input_grad(slot, next_x, next_grad, returned)
    return passed[None, None], weight_out[None], gain_out


def solution(mesh):
    return jax.shard_map(
        per_device,
        mesh=mesh,
        in_specs=(
            P("section", "dp", "fsdp", None),
            P("section", "dp", "fsdp", None),
            P("section", "dp", "fsdp", None),
            P("section", "fsdp", None),
            P("section", "fsdp"),
            P("section", "dp", "fsdp", None),
        ),
        out_specs=(
            P("section", "dp", "fsdp", None),
            P("section", ("fsdp", "dp"), None),
            P("section", ("fsdp", "dp")),
        ),
        check_vma=False,
    )
```

```python
import functools

import jax
import jax.numpy as jnp
from jax import lax
from jax.experimental import pallas as pl
from jax.experimental.pallas import tpu as pltpu
from jax.sharding import PartitionSpec as P

DH = 128
MEM = 128
NEG_FILL = -1e30
EPSILON = 1e-05
LOG2E = 1.4426950408889634
TILE = 16
MIB = 1024 * 1024

SCALAR = pl.BlockSpec(memory_space=pltpu.SMEM)
PARAMS = pltpu.CompilerParams(vmem_limit_bytes=16 * MIB)


def section_route(distance):
    count = lax.axis_size("section")
    return [(s, (s + distance) % count) for s in range(count)]


def along_line(block, distance, wrap=False, odd=None):
    sections, count = lax.axis_size("section"), lax.axis_size("fsdp")
    route = [
        (s * count + f, s * count + (f + distance) % count)
        for s in range(sections)
        for f in range(count)
        if (odd is None or s % 2 == odd) and (wrap or 0 <= f + distance < count)
    ]
    return lax.ppermute(block, ("section", "fsdp"), route)


def to_tokens_below(block, distance):
    sections, count = lax.axis_size("section"), lax.axis_size("fsdp")
    route = [
        (s * count + f, ((s - 1) % sections) * count + (f - distance) % count)
        for s in range(sections)
        for f in range(count)
    ]
    return lax.ppermute(block, ("section", "fsdp"), route)


def after(arrays, others):
    kept, _ = lax.optimization_barrier((arrays, others))
    return kept


def fixed(shape):
    return pl.BlockSpec(shape, lambda *_: (0, 0))


def in_hbm(*arrays):
    return [pltpu.with_memory_space_constraint(array, pltpu.HBM) for array in arrays]


def attention_kernel(count, group, slot_ref, query_ref, grad_ref, *refs):
    key_refs, out_refs = refs[:count], refs[count:]
    rows = query_ref.shape[0]
    slot = slot_ref[0]
    heads = [slice(h * DH, (h + 1) * DH) for h in range(group)]
    query = jnp.concatenate([query_ref[:, h] for h in heads], axis=0)
    grad = jnp.concatenate([grad_ref[:, h] for h in heads], axis=0)
    keys = jnp.concatenate([ref[...] for ref in key_refs], axis=0)
    scores = lax.dot_general(
        keys, query, (((1,), (1,)), ((), ())), preferred_element_type=jnp.float32
    )
    key_at = lax.broadcasted_iota(jnp.int32, (rows, rows), 0)
    query_at = lax.broadcasted_iota(jnp.int32, (rows, rows), 1)
    visible = (key_at <= query_at) | (slot * rows + key_at < MEM)
    visible = jnp.concatenate([visible] * group, axis=1)
    parts = [jnp.where(visible, scores[:rows], NEG_FILL)]
    parts += [scores[d * rows : (d + 1) * rows] for d in range(1, count)]
    hidden = [jnp.where(slot >= d, 0.0, NEG_FILL) for d in range(count)]
    tops = [jnp.max(part, axis=0, keepdims=True) + hide for part, hide in zip(parts, hidden)]
    top = functools.reduce(jnp.maximum, tops)
    scale = DH ** (-0.5) * LOG2E
    weights = [jnp.exp2((part - (top - hide)) * scale) for part, hide in zip(parts, hidden)]
    total = functools.reduce(
        jnp.add, [jnp.sum(weight, axis=0, keepdims=True) for weight in weights]
    )
    inverse = 1.0 / total
    probs = jnp.concatenate([(w * inverse).astype(jnp.bfloat16) for w in weights], axis=0)
    values = jnp.dot(probs, grad, preferred_element_type=jnp.float32)
    for d in range(count):
        out_refs[d][...] = values[d * rows : (d + 1) * rows].astype(jnp.bfloat16)


def attention(slot, queries, grads, key_blocks):
    rows, kv_width = key_blocks[0].shape
    group = queries.shape[1] // kv_width
    count = len(key_blocks)
    wide = pl.BlockSpec((rows, group * DH), lambda g: (0, g))
    narrow = pl.BlockSpec((rows, DH), lambda g: (0, g))
    return pl.pallas_call(
        functools.partial(attention_kernel, count, group),
        grid=(kv_width // DH,),
        in_specs=[SCALAR, wide, wide] + [narrow] * count,
        out_specs=[narrow] * count,
        out_shape=[jax.ShapeDtypeStruct((rows, kv_width), jnp.bfloat16)] * count,
        compiler_params=pltpu.CompilerParams(vmem_limit_bytes=(8 + 3 * count) * MIB),
    )(slot, *in_hbm(queries, grads, *key_blocks))


def prepare_kernel(count, slot_ref, x_ref, grad_ref, pair_ref, *xhat_refs):
    pair_ref[0] = x_ref[...]
    pair_ref[1] = grad_ref[...]
    x = x_ref[...].astype(jnp.float32)
    inv_rms = lax.rsqrt(jnp.mean(x * x, axis=1, keepdims=True) + EPSILON)
    width = x.shape[1] // count
    for d in range(count):
        start = pl.multiple_of(lax.rem(slot_ref[0] + d, count) * width, width)
        block = x_ref[:, pl.ds(start, width)].astype(jnp.float32)
        xhat_refs[d][...] = (block * inv_rms).astype(jnp.bfloat16)


def prepare(slot, x, grads, count):
    rows, width = x.shape
    step = min(rows, 2 * TILE)
    wide = pl.BlockSpec((step, width), lambda r: (r, 0))
    out = pl.pallas_call(
        functools.partial(prepare_kernel, count),
        grid=(rows // step,),
        in_specs=[SCALAR, wide, wide],
        out_specs=[pl.BlockSpec((2, step, width), lambda r: (0, r, 0))]
        + [pl.BlockSpec((step, width // count), lambda r: (r, 0))] * count,
        out_shape=[jax.ShapeDtypeStruct((2, rows, width), jnp.bfloat16)]
        + [jax.ShapeDtypeStruct((rows, width // count), jnp.bfloat16)] * count,
        compiler_params=PARAMS,
    )(slot, *in_hbm(x, grads))
    return out[0], out[1:]


def normed_kernel(count, slot_ref, half_ref, gain_ref, own_ref, *refs):
    above, below, out_ref = refs[: count - 1], refs[count - 1 : -1], refs[-1]
    rows = own_ref.shape[0]
    gain = gain_ref[...].astype(jnp.float32)
    for d in range(count):
        xhat = own_ref[...]
        if d > 0:
            xhat = jnp.where(slot_ref[0] >= d, above[d - 1][...], below[d - 1][...])
        normed = (xhat.astype(jnp.float32) * gain).astype(jnp.bfloat16)
        out_ref[:, d * rows : (d + 1) * rows] = normed.T


def normed_columns(slot, half, halves, gain, own, above, below):
    count = len(above) + 1
    rows, width = own.shape
    width = width // halves
    step = min(width, 256)
    steps = width // step

    def place(c, slot_ref, half_ref):
        return (0, half_ref[0] * steps + c)

    return pl.pallas_call(
        functools.partial(normed_kernel, count),
        grid_spec=pltpu.PrefetchScalarGridSpec(
            num_scalar_prefetch=2,
            grid=(steps,),
            in_specs=[pl.BlockSpec((1, step), place)]
            + [pl.BlockSpec((rows, step), place)] * (2 * count - 1),
            out_specs=pl.BlockSpec((step, count * rows), lambda c, *_: (c, 0)),
        ),
        out_shape=jax.ShapeDtypeStruct((width, count * rows), jnp.bfloat16),
        compiler_params=PARAMS,
    )(slot, half, *in_hbm(gain, own, *above, *below))


def feature_kernel(count, weight_ref, gain_ref, *refs):
    value_refs, scaled_refs, all_ref = refs[:count], refs[count:-1], refs[-1]
    rows = value_refs[0].shape[0]
    values = jnp.concatenate([ref[...] for ref in value_refs], axis=0)

    @pl.when(pl.program_id(0) == 0)
    def _():
        all_ref[...] = values

    normed_grad = lax.dot_general(
        values, weight_ref[...], (((1,), (1,)), ((), ())), preferred_element_type=jnp.float32
    )
    gain = gain_ref[...].astype(jnp.float32)
    for d in range(count):
        scaled_refs[d][...] = (normed_grad[d * rows : (d + 1) * rows] * gain).astype(jnp.bfloat16)


def feature_grads(weight, gain, values):
    count = len(values)
    rows, kv_width = values[0].shape
    width = weight.shape[0]
    step = min(width, 256)
    column = pl.BlockSpec((rows, step), lambda c: (0, c))
    out = pl.pallas_call(
        functools.partial(feature_kernel, count),
        grid=(width // step,),
        in_specs=[
            pl.BlockSpec((step, kv_width), lambda c: (c, 0)),
            pl.BlockSpec((1, step), lambda c: (0, c)),
        ]
        + [fixed((rows, kv_width))] * count,
        out_specs=[column] * count + [fixed((count * rows, kv_width))],
        out_shape=[jax.ShapeDtypeStruct((rows, width), jnp.bfloat16)] * count
        + [jax.ShapeDtypeStruct((count * rows, kv_width), jnp.bfloat16)],
        compiler_params=PARAMS,
    )(*in_hbm(weight, gain, *values))
    return out[:count], out[count]


def weight_kernel(docs, half_ref, weight_ref, gain_ref, *refs):
    normed_refs, value_refs, (out_ref, line_ref) = refs[:docs], refs[docs:-2], refs[-2:]
    normed = jnp.concatenate([ref[...] for ref in normed_refs], axis=1)
    values = jnp.concatenate([ref[...] for ref in value_refs], axis=0)
    grad = jnp.dot(normed, values, preferred_element_type=jnp.float32)
    kv_width = grad.shape[1]
    out_ref[...] = grad.astype(jnp.bfloat16)
    terms = grad * weight_ref[...].astype(jnp.float32)
    lanes = sum(terms[:, i : i + DH] for i in range(0, kv_width, DH))
    line_ref[...] = jnp.sum(lanes.T, axis=0, keepdims=True) / gain_ref[...].astype(jnp.float32)


def weight_grad(half, weight, gain, normed, values):
    docs = len(normed)
    blocks = [block for doc in values for block in doc]
    rows, kv_width = values[0][0].shape
    width, tokens = normed[0].shape
    step = min(width, 256)
    steps = width // step
    return pl.pallas_call(
        functools.partial(weight_kernel, docs),
        grid_spec=pltpu.PrefetchScalarGridSpec(
            num_scalar_prefetch=1,
            grid=(steps,),
            in_specs=[
                pl.BlockSpec((step, kv_width), lambda c, half_ref: (half_ref[0] * steps + c, 0)),
                pl.BlockSpec((1, step), lambda c, half_ref: (0, half_ref[0] * steps + c)),
            ]
            + [pl.BlockSpec((step, tokens), lambda c, *_: (c, 0))] * docs
            + [fixed((rows, kv_width))] * len(blocks),
            out_specs=[
                pl.BlockSpec((step, kv_width), lambda c, *_: (c, 0)),
                pl.BlockSpec((1, step), lambda c, *_: (0, c)),
            ],
        ),
        out_shape=[
            jax.ShapeDtypeStruct((width, kv_width), jnp.bfloat16),
            jax.ShapeDtypeStruct((1, width), jnp.float32),
        ],
        compiler_params=PARAMS,
    )(half, *in_hbm(weight, gain, *normed, *blocks))


def input_kernel(count, slot_ref, pair_ref, *refs):
    scaled_refs, out_ref = refs[:count], refs[count]
    slot = slot_ref[0]
    x_ref, grad_ref = pair_ref.at[0], pair_ref.at[1]
    x = x_ref[...].astype(jnp.float32)
    inv_rms = lax.rsqrt(jnp.mean(x * x, axis=1, keepdims=True) + EPSILON)
    width = x.shape[1] // count
    starts = [pl.multiple_of(lax.rem(slot + d, count) * width, width) for d in range(count)]
    inner = jnp.zeros_like(inv_rms)
    for d in range(count):
        block = x_ref[:, pl.ds(starts[d], width)].astype(jnp.float32)
        inner += jnp.sum(scaled_refs[d][...].astype(jnp.float32) * block, axis=1, keepdims=True)
    inner = inner * inv_rms * inv_rms / x.shape[1]
    for d in range(count):
        columns = pl.ds(starts[d], width)
        block = x_ref[:, columns].astype(jnp.float32)
        scaled = scaled_refs[d][...].astype(jnp.float32)
        grad = grad_ref[:, columns].astype(jnp.float32)
        out_ref[:, columns] = (grad + inv_rms * (scaled - block * inner)).astype(jnp.bfloat16)


def input_grad(slot, pair, scaled):
    count = len(scaled)
    _, rows, width = pair.shape
    step = min(rows, 2 * TILE)
    return pl.pallas_call(
        functools.partial(input_kernel, count),
        grid=(rows // step,),
        in_specs=[SCALAR, pl.BlockSpec((2, step, width), lambda r: (0, r, 0))]
        + [pl.BlockSpec((step, width // count), lambda r: (r, 0))] * count,
        out_specs=pl.BlockSpec((step, width), lambda r: (r, 0)),
        out_shape=jax.ShapeDtypeStruct((rows, width), jnp.bfloat16),
        compiler_params=PARAMS,
    )(slot, *in_hbm(pair, *scaled))


def per_device(section_inputs, queries, keys, w_value, gain, section_grads_in):
    count = lax.axis_size("fsdp")
    docs = lax.axis_size("dp")
    slot = lax.axis_index("fsdp").astype(jnp.int32)[None]
    half = lax.axis_index("dp").astype(jnp.int32)[None]
    x, cotangent, own_keys = section_inputs[0, 0], section_grads_in[0, 0], keys[0, 0]
    weight = w_value[0]
    assert MEM <= x.shape[0] and docs == 2
    distances = range(1, count)

    swap = [(0, 1), (1, 0)]

    pair, xhat = prepare(slot, x, cotangent, count)
    keys_in = [along_line(own_keys, d) for d in distances]
    below = [along_line(xhat[d], d - count) for d in distances[1:]]
    below, keys_in, xhat, slot = after((below, keys_in, xhat, slot), ())
    far_below, far_above = along_line(xhat[1], 1 - count), along_line(xhat[-1], count - 1)
    terms = attention(slot, queries[0, 0], cotangent, [own_keys] + keys_in)

    below = [far_below] + below
    terms, below, far_above, xhat = after((terms, below, far_above, xhat), ())
    arrived = [along_line(terms[d], -d) for d in distances]
    above = [along_line(xhat[d], d) for d in distances[:-1]] + [far_above]
    arrived, above = after((arrived, above), ())
    value = sum(t.astype(jnp.float32) for t in [terms[0]] + arrived).astype(jnp.bfloat16)

    value, pair = after((value, pair), ())
    values = [value] + [along_line(value, d, wrap=True) for d in distances]
    next_pair = lax.ppermute(pair, "section", section_route(-1))
    columns = (docs, gain, after(xhat[0], values[1]), above, below)
    sent = normed_columns(slot, 1 - half, *columns)
    normed = [normed_columns(slot, half, *columns), lax.ppermute(sent, "dp", swap)]
    values, normed, next_pair = after((values, normed, next_pair), ())

    scaled, all_values = feature_grads(weight, gain, values)
    other_values = lax.ppermute(all_values, "dp", swap)
    returned = [to_tokens_below(scaled[d], d) for d in range(count)]

    weight_out, gain_out = weight_grad(half, weight, gain, normed, [[all_values], [other_values]])
    slot = after(slot, weight_out)
    passed = input_grad(slot, next_pair, returned)
    return passed[None, None], weight_out[None], gain_out


def solution(mesh):
    return jax.shard_map(
        per_device,
        mesh=mesh,
        in_specs=(
            P("section", "dp", "fsdp", None),
            P("section", "dp", "fsdp", None),
            P("section", "dp", "fsdp", None),
            P("section", "fsdp", None),
            P("section", "fsdp"),
            P("section", "dp", "fsdp", None),
        ),
        out_specs=(
            P("section", "dp", "fsdp", None),
            P("section", ("fsdp", "dp"), None),
            P("section", ("fsdp", "dp")),
        ),
        check_vma=False,
    )
```

```python
import functools

import jax
import jax.numpy as jnp
from jax import lax
from jax.experimental import pallas as pl
from jax.experimental.pallas import tpu as pltpu
from jax.sharding import PartitionSpec as P

DH = 128
MEM = 128
NEG_FILL = -1e30
EPSILON = 1e-05
LOG2E = 1.4426950408889634
TILE = 16
MIB = 1024 * 1024

SCALAR = pl.BlockSpec(memory_space=pltpu.SMEM)
PARAMS = pltpu.CompilerParams(vmem_limit_bytes=16 * MIB)


def section_route(distance):
    count = lax.axis_size("section")
    return [(s, (s + distance) % count) for s in range(count)]


def to_partner(block, mask, below=False):
    sections, count = lax.axis_size("section"), lax.axis_size("fsdp")
    route = [
        (s * count + f, (s - below) % sections * count + (f ^ mask))
        for s in range(sections)
        for f in range(count)
    ]
    return lax.ppermute(block, ("section", "fsdp"), route)


def after(arrays, others):
    kept, _ = lax.optimization_barrier((arrays, others))
    return kept


def fixed(shape):
    return pl.BlockSpec(shape, lambda *_: (0, 0))


def in_hbm(*arrays):
    return [pltpu.with_memory_space_constraint(array, pltpu.HBM) for array in arrays]


def attention_kernel(count, group, heads, x_steps, slot_ref, query_ref, grad_ref, *refs):
    key_refs, x_refs, out_refs = refs[:count], refs[count : -count], refs[-count:]
    rows = query_ref.shape[0]
    slot = slot_ref[0]
    key_at = lax.broadcasted_iota(jnp.int32, (rows, rows), 0)
    query_at = lax.broadcasted_iota(jnp.int32, (rows, rows), 1)
    visible = (key_at <= query_at) | (slot * rows + key_at < MEM)
    visible = jnp.concatenate([visible] * group, axis=1)
    hidden = [0.0] + [jnp.where(slot ^ m < slot, 0.0, NEG_FILL) for m in range(1, count)]
    scale = DH ** (-0.5) * LOG2E
    for head in range(heads):
        own = slice(head * DH, (head + 1) * DH)
        members = [slice(h * DH, (h + 1) * DH) for h in range(head * group, (head + 1) * group)]
        query = jnp.concatenate([query_ref[:, h] for h in members], axis=0)
        grad = jnp.concatenate([grad_ref[:, h] for h in members], axis=0)
        keys = jnp.concatenate([ref[:, own] for ref in key_refs], axis=0)
        scores = lax.dot_general(
            keys, query, (((1,), (1,)), ((), ())), preferred_element_type=jnp.float32
        )
        parts = [scores[m * rows : (m + 1) * rows] for m in range(count)]
        parts[0] = jnp.where(visible, parts[0], NEG_FILL)
        tops = [jnp.max(part, axis=0, keepdims=True) + hide for part, hide in zip(parts, hidden)]
        top = functools.reduce(jnp.maximum, tops)
        weights = [jnp.exp2((part - (top - hide)) * scale) for part, hide in zip(parts, hidden)]
        sums = [jnp.sum(weight, axis=0, keepdims=True) for weight in weights]
        inverse = 1.0 / functools.reduce(jnp.add, sums)
        probs = jnp.concatenate([(w * inverse).astype(jnp.bfloat16) for w in weights], axis=0)
        values = jnp.dot(probs, grad, preferred_element_type=jnp.float32)
        for m in range(count):
            out_refs[m][:, own] = values[m * rows : (m + 1) * rows].astype(jnp.bfloat16)
    for m in range(1, count):

        @pl.when((slot ^ m > slot) & (pl.program_id(0) < x_steps))
        def _():
            out_refs[m][...] = x_refs[m - 1][...]


def attention(slot, queries, grads, key_blocks, x):
    rows, kv_width = key_blocks[0].shape
    group = queries.shape[1] // kv_width
    count = len(key_blocks)
    x_width = x.shape[1] // count
    heads = min(4, kv_width // DH) if count <= 4 else 1
    width = heads * DH
    x_steps = x_width // width
    assert x_width <= kv_width and x_width % width == 0
    wide = pl.BlockSpec((rows, group * width), lambda g, _: (0, g))
    narrow = pl.BlockSpec((rows, width), lambda g, _: (0, g))
    columns = [
        pl.BlockSpec(
            (rows, width),
            lambda g, ref, m=m: (0, (ref[0] ^ m) * x_steps + jnp.minimum(g, x_steps - 1)),
        )
        for m in range(1, count)
    ]
    return pl.pallas_call(
        functools.partial(attention_kernel, count, group, heads, x_steps),
        grid_spec=pltpu.PrefetchScalarGridSpec(
            num_scalar_prefetch=1,
            grid=(kv_width // width,),
            in_specs=[wide, wide] + [narrow] * count + columns,
            out_specs=[narrow] * count,
        ),
        out_shape=[jax.ShapeDtypeStruct((rows, kv_width), jnp.bfloat16)] * count,
        compiler_params=pltpu.CompilerParams(vmem_limit_bytes=(24 + 2 * count) * MIB),
    )(slot, *in_hbm(queries, grads, *key_blocks, *[x] * (count - 1)))


def rms_kernel(x_ref, out_ref):
    x = x_ref[...].astype(jnp.float32)
    inv_rms = lax.rsqrt(jnp.mean(x * x, axis=1, keepdims=True) + EPSILON)
    out_ref[...] = jnp.broadcast_to(inv_rms, out_ref.shape)


def inverse_rms(x):
    rows, width = x.shape
    step = min(rows, 2 * TILE)
    return pl.pallas_call(
        rms_kernel,
        grid=(rows // step,),
        in_specs=[pl.BlockSpec((step, width), lambda r: (r, 0))],
        out_specs=pl.BlockSpec((step, DH), lambda r: (r, 0)),
        out_shape=jax.ShapeDtypeStruct((rows, DH), jnp.float32),
        compiler_params=PARAMS,
    )(*in_hbm(x))


def value_kernel(count, slot_ref, rms_ref, own_ref, *refs):
    slot = slot_ref[0]
    total = own_ref[...].astype(jnp.float32)
    for m in range(1, count):
        total += jnp.where(slot ^ m > slot, refs[m - 1][...].astype(jnp.float32), 0.0)
    refs[-1][...] = (total * rms_ref[:, :1]).astype(jnp.bfloat16)


def value_grad(slot, inv_rms, own_term, received):
    rows, width = own_term.shape
    step = min(rows, 4 * TILE)
    line = pl.BlockSpec((step, width), lambda r: (r, 0))
    return pl.pallas_call(
        functools.partial(value_kernel, len(received) + 1),
        grid=(rows // step,),
        in_specs=[SCALAR, pl.BlockSpec((step, DH), lambda r: (r, 0))]
        + [line] * (len(received) + 1),
        out_specs=line,
        out_shape=jax.ShapeDtypeStruct((rows, width), jnp.bfloat16),
        compiler_params=PARAMS,
    )(slot, *in_hbm(inv_rms, own_term, *received))


def column_kernel(count, slot_ref, half_ref, gain_ref, own_ref, *refs):
    first, second, out_ref = refs[: count - 1], refs[count - 1 : -1], refs[-1]
    slot = slot_ref[0]
    rows = own_ref.shape[0]
    gain = gain_ref[...].astype(jnp.float32)
    for m in range(count):
        x = own_ref[...]
        if m > 0:
            x = jnp.where(slot ^ m > slot, first[m - 1][...], second[m - 1][...])
        out_ref[:, m * rows : (m + 1) * rows] = (x.astype(jnp.float32) * gain).astype(jnp.bfloat16).T


def gained_columns(slot, half, halves, gain, x, first, second):
    count = len(first) + 1
    rows, width = x.shape
    width = width // count // halves
    step = min(width, 256)
    steps = width // step

    def place(c, slot_ref, half_ref):
        return (0, half_ref[0] * steps + c)

    def own_place(c, slot_ref, half_ref):
        return (0, (slot_ref[0] * halves + half_ref[0]) * steps + c)

    return pl.pallas_call(
        functools.partial(column_kernel, count),
        grid_spec=pltpu.PrefetchScalarGridSpec(
            num_scalar_prefetch=2,
            grid=(steps,),
            in_specs=[pl.BlockSpec((1, step), place), pl.BlockSpec((rows, step), own_place)]
            + [pl.BlockSpec((rows, step), place)] * (2 * count - 2),
            out_specs=pl.BlockSpec((step, count * rows), lambda c, *_: (c, 0)),
        ),
        out_shape=jax.ShapeDtypeStruct((width, count * rows), jnp.bfloat16),
        compiler_params=PARAMS,
    )(slot, half, *in_hbm(gain, x, *first, *second))


def feature_kernel(count, weight_ref, gain_ref, *refs):
    value_refs, scaled_refs, all_ref = refs[:count], refs[count:-1], refs[-1]
    rows = value_refs[0].shape[0]
    values = jnp.concatenate([ref[...] for ref in value_refs], axis=0)

    @pl.when(pl.program_id(0) == 0)
    def _():
        all_ref[...] = values

    normed_grad = lax.dot_general(
        values, weight_ref[...], (((1,), (1,)), ((), ())), preferred_element_type=jnp.float32
    )
    gain = gain_ref[...].astype(jnp.float32)
    for d in range(count):
        scaled_refs[d][...] = (normed_grad[d * rows : (d + 1) * rows] * gain).astype(jnp.bfloat16)


def feature_grads(weight, gain, values):
    count = len(values)
    rows, kv_width = values[0].shape
    width = weight.shape[0]
    step = min(width, 1024)
    column = pl.BlockSpec((rows, step), lambda c: (0, c))
    out = pl.pallas_call(
        functools.partial(feature_kernel, count),
        grid=(width // step,),
        in_specs=[
            pl.BlockSpec((step, kv_width), lambda c: (c, 0)),
            pl.BlockSpec((1, step), lambda c: (0, c)),
        ]
        + [fixed((rows, kv_width))] * count,
        out_specs=[column] * count + [fixed((count * rows, kv_width))],
        out_shape=[jax.ShapeDtypeStruct((rows, width), jnp.bfloat16)] * count
        + [jax.ShapeDtypeStruct((count * rows, kv_width), jnp.bfloat16)],
        compiler_params=PARAMS,
    )(*in_hbm(weight, gain, *values))
    return out[:count], out[count]


def weight_kernel(docs, half_ref, weight_ref, gain_ref, *refs):
    normed_refs, value_refs, (out_ref, line_ref) = refs[:docs], refs[docs:-2], refs[-2:]
    normed = jnp.concatenate([ref[...] for ref in normed_refs], axis=1)
    values = jnp.concatenate([ref[...] for ref in value_refs], axis=0)
    grad = jnp.dot(normed, values, preferred_element_type=jnp.float32)
    kv_width = grad.shape[1]
    out_ref[...] = grad.astype(jnp.bfloat16)
    terms = grad * weight_ref[...].astype(jnp.float32)
    lanes = sum(terms[:, i : i + DH] for i in range(0, kv_width, DH))
    line_ref[...] = jnp.sum(lanes.T, axis=0, keepdims=True) / gain_ref[...].astype(jnp.float32)


def weight_grad(half, weight, gain, normed, values):
    docs = len(normed)
    blocks = [block for doc in values for block in doc]
    rows, kv_width = values[0][0].shape
    width, tokens = normed[0].shape
    step = min(width, 256)
    steps = width // step
    return pl.pallas_call(
        functools.partial(weight_kernel, docs),
        grid_spec=pltpu.PrefetchScalarGridSpec(
            num_scalar_prefetch=1,
            grid=(steps,),
            in_specs=[
                pl.BlockSpec((step, kv_width), lambda c, half_ref: (half_ref[0] * steps + c, 0)),
                pl.BlockSpec((1, step), lambda c, half_ref: (0, half_ref[0] * steps + c)),
            ]
            + [pl.BlockSpec((step, tokens), lambda c, *_: (c, 0))] * docs
            + [fixed((rows, kv_width))] * len(blocks),
            out_specs=[
                pl.BlockSpec((step, kv_width), lambda c, *_: (c, 0)),
                pl.BlockSpec((1, step), lambda c, *_: (0, c)),
            ],
        ),
        out_shape=[
            jax.ShapeDtypeStruct((width, kv_width), jnp.bfloat16),
            jax.ShapeDtypeStruct((1, width), jnp.float32),
        ],
        compiler_params=PARAMS,
    )(half, *in_hbm(weight, gain, *normed, *blocks))


def input_kernel(count, slot_ref, x_ref, grad_ref, *refs):
    scaled_refs, out_ref = refs[:count], refs[count]
    slot = slot_ref[0]
    x = x_ref[...].astype(jnp.float32)
    square = 1.0 / (jnp.mean(x * x, axis=1, keepdims=True) + EPSILON)
    width = x.shape[1] // count
    starts = [pl.multiple_of((slot ^ m) * width, width) for m in range(count)]
    inner = jnp.zeros_like(square)
    for m in range(count):
        block = x_ref[:, pl.ds(starts[m], width)].astype(jnp.float32)
        inner += jnp.sum(scaled_refs[m][...].astype(jnp.float32) * block, axis=1, keepdims=True)
    inner = inner * square / x.shape[1]
    for m in range(count):
        columns = pl.ds(starts[m], width)
        block = x_ref[:, columns].astype(jnp.float32)
        grad = grad_ref[:, columns].astype(jnp.float32)
        scaled = scaled_refs[m][...].astype(jnp.float32)
        out_ref[:, columns] = (grad + (scaled - block * inner)).astype(jnp.bfloat16)


def input_grad(slot, x, grads, scaled):
    count = len(scaled)
    rows, width = x.shape
    step = min(rows, 4 * TILE)
    wide = pl.BlockSpec((step, width), lambda r: (r, 0))
    return pl.pallas_call(
        functools.partial(input_kernel, count),
        grid=(rows // step,),
        in_specs=[SCALAR, wide, wide]
        + [pl.BlockSpec((step, width // count), lambda r: (r, 0))] * count,
        out_specs=wide,
        out_shape=jax.ShapeDtypeStruct((rows, width), jnp.bfloat16),
        compiler_params=PARAMS,
    )(slot, *in_hbm(x, grads, *scaled))


def per_device(section_inputs, queries, keys, w_value, gain, section_grads_in):
    count = lax.axis_size("fsdp")
    docs = lax.axis_size("dp")
    slot = lax.axis_index("fsdp").astype(jnp.int32)[None]
    half = lax.axis_index("dp").astype(jnp.int32)[None]
    x, cotangent, own_keys = section_inputs[0, 0], section_grads_in[0, 0], keys[0, 0]
    weight = w_value[0]
    assert MEM <= x.shape[0] and docs == 2 and count & (count - 1) == 0
    masks = range(1, count)

    swap = [(0, 1), (1, 0)]

    x_width = x.shape[1] // count
    first = []
    for m in masks:
        columns = lax.dynamic_slice_in_dim(x, (slot[0] ^ m) * x_width, x_width, axis=1)
        columns = jnp.pad(columns, ((0, 0), (0, own_keys.shape[1] - x_width)))
        first.append(to_partner(jnp.where(slot[0] ^ m > slot[0], own_keys, columns), m))
    next_x = lax.ppermute(x, "section", section_route(-1))
    inv_rms = inverse_rms(x)
    first, next_x, inv_rms, slot = after((first, next_x, inv_rms, slot), ())
    terms = attention(slot, queries[0, 0], cotangent, [own_keys] + first, x)

    second = [to_partner(terms[m], m) for m in masks]
    next_grad = lax.ppermute(after(cotangent, terms), "section", section_route(-1))
    second, next_grad = after((second, next_grad), ())
    value = value_grad(slot, inv_rms, terms[0], second)
    sent = gained_columns(slot, 1 - half, docs, gain, x, first, second)

    value, sent = after((value, sent), ())
    values = [value] + [to_partner(value, m) for m in masks]
    normed = [
        gained_columns(slot, half, docs, gain, x, first, second),
        lax.ppermute(sent, "dp", swap),
    ]
    values, normed = after((values, normed), ())

    scaled, all_values = feature_grads(weight, gain, values)
    other_values = lax.ppermute(all_values, "dp", swap)
    returned = [to_partner(scaled[m], m, below=True) for m in range(count)]

    weight_out, gain_out = weight_grad(half, weight, gain, normed, [[all_values], [other_values]])
    slot = after(slot, weight_out)
    passed = input_grad(slot, next_x, next_grad, returned)
    return passed[None, None], weight_out[None], gain_out


def solution(mesh):
    return jax.shard_map(
        per_device,
        mesh=mesh,
        in_specs=(
            P("section", "dp", "fsdp", None),
            P("section", "dp", "fsdp", None),
            P("section", "dp", "fsdp", None),
            P("section", "fsdp", None),
            P("section", "fsdp"),
            P("section", "dp", "fsdp", None),
        ),
        out_specs=(
            P("section", "dp", "fsdp", None),
            P("section", ("fsdp", "dp"), None),
            P("section", ("fsdp", "dp")),
        ),
        check_vma=False,
    )
```

```python
import functools

import jax
import jax.numpy as jnp
from jax import lax
from jax.experimental import pallas as pl
from jax.experimental.pallas import tpu as pltpu
from jax.sharding import PartitionSpec as P

DH = 128
MEM = 128
NEG_FILL = -1e30
EPSILON = 1e-05
LOG2E = 1.4426950408889634
TILE = 16
MIB = 1024 * 1024

SCALAR = pl.BlockSpec(memory_space=pltpu.SMEM)
PARAMS = pltpu.CompilerParams(vmem_limit_bytes=16 * MIB)


def section_route(distance):
    count = lax.axis_size("section")
    return [(s, (s + distance) % count) for s in range(count)]


def to_partner(block, mask, below=False):
    sections, count = lax.axis_size("section"), lax.axis_size("fsdp")
    route = [
        (s * count + f, (s - below) % sections * count + (f ^ mask))
        for s in range(sections)
        for f in range(count)
    ]
    return lax.ppermute(block, ("section", "fsdp"), route)


def after(arrays, others):
    kept, _ = lax.optimization_barrier((arrays, others))
    return kept


def fixed(shape):
    return pl.BlockSpec(shape, lambda *_: (0, 0))


def in_hbm(*arrays):
    return [pltpu.with_memory_space_constraint(array, pltpu.HBM) for array in arrays]


def attention_kernel(count, group, heads, x_steps, slot_ref, query_ref, grad_ref, *refs):
    key_refs, x_refs, out_refs = refs[:count], refs[count : -count], refs[-count:]
    rows = query_ref.shape[0]
    slot = slot_ref[0]
    key_at = lax.broadcasted_iota(jnp.int32, (rows, rows), 0)
    query_at = lax.broadcasted_iota(jnp.int32, (rows, rows), 1)
    visible = (key_at <= query_at) | (slot * rows + key_at < MEM)
    visible = jnp.concatenate([visible] * group, axis=1)
    hidden = [0.0] + [jnp.where(slot ^ m < slot, 0.0, NEG_FILL) for m in range(1, count)]
    scale = DH ** (-0.5) * LOG2E
    for head in range(heads):
        own = slice(head * DH, (head + 1) * DH)
        members = [slice(h * DH, (h + 1) * DH) for h in range(head * group, (head + 1) * group)]
        query = jnp.concatenate([query_ref[:, h] for h in members], axis=0)
        grad = jnp.concatenate([grad_ref[:, h] for h in members], axis=0)
        keys = jnp.concatenate([ref[:, own] for ref in key_refs], axis=0)
        scores = lax.dot_general(
            keys, query, (((1,), (1,)), ((), ())), preferred_element_type=jnp.float32
        )
        parts = [scores[m * rows : (m + 1) * rows] for m in range(count)]
        parts[0] = jnp.where(visible, parts[0], NEG_FILL)
        tops = [jnp.max(part, axis=0, keepdims=True) + hide for part, hide in zip(parts, hidden)]
        top = functools.reduce(jnp.maximum, tops)
        weights = [jnp.exp2((part - (top - hide)) * scale) for part, hide in zip(parts, hidden)]
        sums = [jnp.sum(weight, axis=0, keepdims=True) for weight in weights]
        inverse = 1.0 / functools.reduce(jnp.add, sums)
        probs = jnp.concatenate([(w * inverse).astype(jnp.bfloat16) for w in weights], axis=0)
        values = jnp.dot(probs, grad, preferred_element_type=jnp.float32)
        for m in range(count):
            out_refs[m][:, own] = values[m * rows : (m + 1) * rows].astype(jnp.bfloat16)
    for m in range(1, count):

        @pl.when((slot ^ m > slot) & (pl.program_id(0) < x_steps))
        def _():
            out_refs[m][...] = x_refs[m - 1][...]


def attention(slot, queries, grads, key_blocks, x):
    rows, kv_width = key_blocks[0].shape
    group = queries.shape[1] // kv_width
    count = len(key_blocks)
    x_width = x.shape[1] // count
    heads = min(4, kv_width // DH) if count <= 4 else 1
    width = heads * DH
    x_steps = x_width // width
    assert x_width <= kv_width and x_width % width == 0
    wide = pl.BlockSpec((rows, group * width), lambda g, _: (0, g))
    narrow = pl.BlockSpec((rows, width), lambda g, _: (0, g))
    columns = [
        pl.BlockSpec(
            (rows, width),
            lambda g, ref, m=m: (0, (ref[0] ^ m) * x_steps + jnp.minimum(g, x_steps - 1)),
        )
        for m in range(1, count)
    ]
    return pl.pallas_call(
        functools.partial(attention_kernel, count, group, heads, x_steps),
        grid_spec=pltpu.PrefetchScalarGridSpec(
            num_scalar_prefetch=1,
            grid=(kv_width // width,),
            in_specs=[wide, wide] + [narrow] * count + columns,
            out_specs=[narrow] * count,
        ),
        out_shape=[jax.ShapeDtypeStruct((rows, kv_width), jnp.bfloat16)] * count,
        compiler_params=pltpu.CompilerParams(vmem_limit_bytes=(24 + 2 * count) * MIB),
    )(slot, *in_hbm(queries, grads, key_blocks[0]), *key_blocks[1:], *in_hbm(*[x] * (count - 1)))


def rms_kernel(x_ref, out_ref):
    x = x_ref[...].astype(jnp.float32)
    inv_rms = lax.rsqrt(jnp.mean(x * x, axis=1, keepdims=True) + EPSILON)
    out_ref[...] = jnp.broadcast_to(inv_rms, out_ref.shape)


def inverse_rms(x):
    rows, width = x.shape
    step = min(rows, 2 * TILE)
    return pl.pallas_call(
        rms_kernel,
        grid=(rows // step,),
        in_specs=[pl.BlockSpec((step, width), lambda r: (r, 0))],
        out_specs=pl.BlockSpec((step, DH), lambda r: (r, 0)),
        out_shape=jax.ShapeDtypeStruct((rows, DH), jnp.float32),
        compiler_params=PARAMS,
    )(*in_hbm(x))


def value_kernel(count, slot_ref, rms_ref, own_ref, *refs):
    slot = slot_ref[0]
    total = own_ref[...].astype(jnp.float32)
    for m in range(1, count):
        total += jnp.where(slot ^ m > slot, refs[m - 1][...].astype(jnp.float32), 0.0)
    refs[-1][...] = (total * rms_ref[:, :1]).astype(jnp.bfloat16)


def value_grad(slot, inv_rms, own_term, received):
    rows, width = own_term.shape
    step = min(rows, 4 * TILE)
    line = pl.BlockSpec((step, width), lambda r: (r, 0))
    return pl.pallas_call(
        functools.partial(value_kernel, len(received) + 1),
        grid=(rows // step,),
        in_specs=[SCALAR, pl.BlockSpec((step, DH), lambda r: (r, 0))]
        + [line] * (len(received) + 1),
        out_specs=line,
        out_shape=jax.ShapeDtypeStruct((rows, width), jnp.bfloat16),
        compiler_params=PARAMS,
    )(slot, inv_rms, own_term, *received)


def column_kernel(count, slot_ref, half_ref, gain_ref, own_ref, *refs):
    first, second, out_ref = refs[: count - 1], refs[count - 1 : -1], refs[-1]
    slot = slot_ref[0]
    rows = own_ref.shape[0]
    gain = gain_ref[...].astype(jnp.float32)
    for m in range(count):
        x = own_ref[...]
        if m > 0:
            x = jnp.where(slot ^ m > slot, first[m - 1][...], second[m - 1][...])
        out_ref[:, m * rows : (m + 1) * rows] = (x.astype(jnp.float32) * gain).astype(jnp.bfloat16).T


def gained_columns(slot, half, halves, gain, x, first, second):
    count = len(first) + 1
    rows, width = x.shape
    width = width // count // halves
    step = min(width, 256)
    steps = width // step

    def place(c, slot_ref, half_ref):
        return (0, half_ref[0] * steps + c)

    def own_place(c, slot_ref, half_ref):
        return (0, (slot_ref[0] * halves + half_ref[0]) * steps + c)

    return pl.pallas_call(
        functools.partial(column_kernel, count),
        grid_spec=pltpu.PrefetchScalarGridSpec(
            num_scalar_prefetch=2,
            grid=(steps,),
            in_specs=[pl.BlockSpec((1, step), place), pl.BlockSpec((rows, step), own_place)]
            + [pl.BlockSpec((rows, step), place)] * (2 * count - 2),
            out_specs=pl.BlockSpec((step, count * rows), lambda c, *_: (c, 0)),
        ),
        out_shape=jax.ShapeDtypeStruct((width, count * rows), jnp.bfloat16),
        compiler_params=PARAMS,
    )(slot, half, *in_hbm(gain, x), *first, *second)


def feature_kernel(count, weight_ref, gain_ref, *refs):
    value_refs, scaled_refs, all_ref = refs[:count], refs[count:-1], refs[-1]
    rows = value_refs[0].shape[0]
    values = jnp.concatenate([ref[...] for ref in value_refs], axis=0)

    @pl.when(pl.program_id(0) == 0)
    def _():
        all_ref[...] = values

    normed_grad = lax.dot_general(
        values, weight_ref[...], (((1,), (1,)), ((), ())), preferred_element_type=jnp.float32
    )
    gain = gain_ref[...].astype(jnp.float32)
    for d in range(count):
        scaled_refs[d][...] = (normed_grad[d * rows : (d + 1) * rows] * gain).astype(jnp.bfloat16)


def feature_grads(weight, gain, values):
    count = len(values)
    rows, kv_width = values[0].shape
    width = weight.shape[0]
    step = min(width, 1024)
    column = pl.BlockSpec((rows, step), lambda c: (0, c))
    out = pl.pallas_call(
        functools.partial(feature_kernel, count),
        grid=(width // step,),
        in_specs=[
            pl.BlockSpec((step, kv_width), lambda c: (c, 0)),
            pl.BlockSpec((1, step), lambda c: (0, c)),
        ]
        + [fixed((rows, kv_width))] * count,
        out_specs=[column] * count + [fixed((count * rows, kv_width))],
        out_shape=[jax.ShapeDtypeStruct((rows, width), jnp.bfloat16)] * count
        + [jax.ShapeDtypeStruct((count * rows, kv_width), jnp.bfloat16)],
        compiler_params=PARAMS,
    )(*in_hbm(weight, gain), *values)
    return out[:count], out[count]


def weight_kernel(docs, half_ref, weight_ref, gain_ref, *refs):
    normed_refs, value_refs, (out_ref, line_ref) = refs[:docs], refs[docs:-2], refs[-2:]
    normed = jnp.concatenate([ref[...] for ref in normed_refs], axis=1)
    values = jnp.concatenate([ref[...] for ref in value_refs], axis=0)
    grad = jnp.dot(normed, values, preferred_element_type=jnp.float32)
    kv_width = grad.shape[1]
    out_ref[...] = grad.astype(jnp.bfloat16)
    terms = grad * weight_ref[...].astype(jnp.float32)
    lanes = sum(terms[:, i : i + DH] for i in range(0, kv_width, DH))
    line_ref[...] = jnp.sum(lanes.T, axis=0, keepdims=True) / gain_ref[...].astype(jnp.float32)


def weight_grad(half, weight, gain, normed, values):
    docs = len(normed)
    blocks = [block for doc in values for block in doc]
    rows, kv_width = values[0][0].shape
    width, tokens = normed[0].shape
    step = min(width, 256)
    steps = width // step
    return pl.pallas_call(
        functools.partial(weight_kernel, docs),
        grid_spec=pltpu.PrefetchScalarGridSpec(
            num_scalar_prefetch=1,
            grid=(steps,),
            in_specs=[
                pl.BlockSpec((step, kv_width), lambda c, half_ref: (half_ref[0] * steps + c, 0)),
                pl.BlockSpec((1, step), lambda c, half_ref: (0, half_ref[0] * steps + c)),
            ]
            + [pl.BlockSpec((step, tokens), lambda c, *_: (c, 0))] * docs
            + [fixed((rows, kv_width))] * len(blocks),
            out_specs=[
                pl.BlockSpec((step, kv_width), lambda c, *_: (c, 0)),
                pl.BlockSpec((1, step), lambda c, *_: (0, c)),
            ],
        ),
        out_shape=[
            jax.ShapeDtypeStruct((width, kv_width), jnp.bfloat16),
            jax.ShapeDtypeStruct((1, width), jnp.float32),
        ],
        compiler_params=PARAMS,
    )(half, *in_hbm(weight, gain), *normed, *blocks)


def input_kernel(count, slot_ref, x_ref, grad_ref, *refs):
    scaled_refs, out_ref = refs[:count], refs[count]
    slot = slot_ref[0]
    x = x_ref[...].astype(jnp.float32)
    square = 1.0 / (jnp.mean(x * x, axis=1, keepdims=True) + EPSILON)
    width = x.shape[1] // count
    starts = [pl.multiple_of((slot ^ m) * width, width) for m in range(count)]
    inner = jnp.zeros_like(square)
    for m in range(count):
        block = x_ref[:, pl.ds(starts[m], width)].astype(jnp.float32)
        inner += jnp.sum(scaled_refs[m][...].astype(jnp.float32) * block, axis=1, keepdims=True)
    inner = inner * square / x.shape[1]
    for m in range(count):
        columns = pl.ds(starts[m], width)
        block = x_ref[:, columns].astype(jnp.float32)
        grad = grad_ref[:, columns].astype(jnp.float32)
        scaled = scaled_refs[m][...].astype(jnp.float32)
        out_ref[:, columns] = (grad + (scaled - block * inner)).astype(jnp.bfloat16)


def input_grad(slot, x, grads, scaled):
    count = len(scaled)
    rows, width = x.shape
    step = min(rows, 4 * TILE)
    wide = pl.BlockSpec((step, width), lambda r: (r, 0))
    return pl.pallas_call(
        functools.partial(input_kernel, count),
        grid=(rows // step,),
        in_specs=[SCALAR, wide, wide]
        + [pl.BlockSpec((step, width // count), lambda r: (r, 0))] * count,
        out_specs=wide,
        out_shape=jax.ShapeDtypeStruct((rows, width), jnp.bfloat16),
        compiler_params=PARAMS,
    )(slot, x, grads, *scaled)


def per_device(section_inputs, queries, keys, w_value, gain, section_grads_in):
    count = lax.axis_size("fsdp")
    docs = lax.axis_size("dp")
    slot = lax.axis_index("fsdp").astype(jnp.int32)[None]
    half = lax.axis_index("dp").astype(jnp.int32)[None]
    x, cotangent, own_keys = section_inputs[0, 0], section_grads_in[0, 0], keys[0, 0]
    weight = w_value[0]
    assert MEM <= x.shape[0] and docs == 2 and count & (count - 1) == 0
    masks = range(1, count)

    swap = [(0, 1), (1, 0)]

    x_width = x.shape[1] // count
    first = []
    for m in masks:
        columns = lax.dynamic_slice_in_dim(x, (slot[0] ^ m) * x_width, x_width, axis=1)
        columns = jnp.pad(columns, ((0, 0), (0, own_keys.shape[1] - x_width)))
        first.append(to_partner(jnp.where(slot[0] ^ m > slot[0], own_keys, columns), m))
    next_x = lax.ppermute(x, "section", section_route(-1))
    inv_rms = inverse_rms(x)
    first, next_x, inv_rms, slot = after((first, next_x, inv_rms, slot), ())
    terms = attention(slot, queries[0, 0], cotangent, [own_keys] + first, x)

    second = [to_partner(terms[m], m) for m in reversed(masks)][::-1]
    next_grad = lax.ppermute(after(cotangent, terms), "section", section_route(-1))
    second, next_grad = after((second, next_grad), ())
    value = value_grad(slot, inv_rms, terms[0], second)
    sent = gained_columns(slot, 1 - half, docs, gain, x, first, second)

    value, sent = after((value, sent), ())
    values = [value] + [to_partner(value, m) for m in masks]
    normed = [
        gained_columns(slot, half, docs, gain, x, first, second),
        lax.ppermute(sent, "dp", swap),
    ]
    values, normed = after((values, normed), ())

    scaled, all_values = feature_grads(weight, gain, values)
    other_values = lax.ppermute(all_values, "dp", swap)
    returned = [to_partner(scaled[m], m, below=True) for m in reversed(range(count))][::-1]

    weight_out, gain_out = weight_grad(half, weight, gain, normed, [[all_values], [other_values]])
    slot = after(slot, weight_out)
    passed = input_grad(slot, next_x, next_grad, returned)
    return passed[None, None], weight_out[None], gain_out


def solution(mesh):
    return jax.shard_map(
        per_device,
        mesh=mesh,
        in_specs=(
            P("section", "dp", "fsdp", None),
            P("section", "dp", "fsdp", None),
            P("section", "dp", "fsdp", None),
            P("section", "fsdp", None),
            P("section", "fsdp"),
            P("section", "dp", "fsdp", None),
        ),
        out_specs=(
            P("section", "dp", "fsdp", None),
            P("section", ("fsdp", "dp"), None),
            P("section", ("fsdp", "dp")),
        ),
        check_vma=False,
    )
```

```python
import functools

import jax
import jax.numpy as jnp
from jax import lax
from jax.experimental import pallas as pl
from jax.experimental.pallas import tpu as pltpu
from jax.sharding import PartitionSpec as P

DH = 128
MEM = 128
NEG_FILL = -1e30
EPSILON = 1e-05
LOG2E = 1.4426950408889634
TILE = 16
MIB = 1024 * 1024

SCALAR = pl.BlockSpec(memory_space=pltpu.SMEM)
PARAMS = pltpu.CompilerParams(vmem_limit_bytes=16 * MIB)


def section_route(distance):
    count = lax.axis_size("section")
    return [(s, (s + distance) % count) for s in range(count)]


def to_partner(block, mask, below=False):
    sections, count = lax.axis_size("section"), lax.axis_size("fsdp")
    route = [
        (s * count + f, (s - below) % sections * count + (f ^ mask))
        for s in range(sections)
        for f in range(count)
    ]
    return lax.ppermute(block, ("section", "fsdp"), route)


def after(arrays, others):
    kept, _ = lax.optimization_barrier((arrays, others))
    return kept


def fixed(shape):
    return pl.BlockSpec(shape, lambda *_: (0, 0))


def in_hbm(*arrays):
    return [pltpu.with_memory_space_constraint(array, pltpu.HBM) for array in arrays]


def attention_kernel(count, group, heads, x_steps, slot_ref, query_ref, grad_ref, *refs):
    key_refs, x_refs = refs[:count], refs[count : 2 * count - 1]
    out_refs, kept_refs = refs[2 * count - 1 : 3 * count - 1], refs[3 * count - 1 :]
    rows = query_ref.shape[0]
    slot = slot_ref[0]
    key_at = lax.broadcasted_iota(jnp.int32, (rows, rows), 0)
    query_at = lax.broadcasted_iota(jnp.int32, (rows, rows), 1)
    visible = (key_at <= query_at) | (slot * rows + key_at < MEM)
    visible = jnp.concatenate([visible] * group, axis=1)
    hidden = [0.0] + [jnp.where(slot ^ m < slot, 0.0, NEG_FILL) for m in range(1, count)]
    scale = DH ** (-0.5) * LOG2E
    for head in range(heads):
        own = slice(head * DH, (head + 1) * DH)
        members = [slice(h * DH, (h + 1) * DH) for h in range(head * group, (head + 1) * group)]
        query = jnp.concatenate([query_ref[:, h] for h in members], axis=0)
        grad = jnp.concatenate([grad_ref[:, h] for h in members], axis=0)
        keys = jnp.concatenate([ref[:, own] for ref in key_refs], axis=0)
        scores = lax.dot_general(
            keys, query, (((1,), (1,)), ((), ())), preferred_element_type=jnp.float32
        )
        parts = [scores[m * rows : (m + 1) * rows] for m in range(count)]
        parts[0] = jnp.where(visible, parts[0], NEG_FILL)
        tops = [jnp.max(part, axis=0, keepdims=True) + hide for part, hide in zip(parts, hidden)]
        top = functools.reduce(jnp.maximum, tops)
        weights = [jnp.exp2((part - (top - hide)) * scale) for part, hide in zip(parts, hidden)]
        sums = [jnp.sum(weight, axis=0, keepdims=True) for weight in weights]
        inverse = 1.0 / functools.reduce(jnp.add, sums)
        probs = jnp.concatenate([(w * inverse).astype(jnp.bfloat16) for w in weights], axis=0)
        values = jnp.dot(probs, grad, preferred_element_type=jnp.float32)
        for m in range(count):
            out_refs[m][:, own] = values[m * rows : (m + 1) * rows].astype(jnp.bfloat16)
    for m in range(1, count):
        kept_refs[m - 1][...] = key_refs[m][...]

        @pl.when((slot ^ m > slot) & (pl.program_id(0) < x_steps))
        def _():
            out_refs[m][...] = x_refs[m - 1][...]


def attention(slot, queries, grads, key_blocks, x):
    rows, kv_width = key_blocks[0].shape
    group = queries.shape[1] // kv_width
    count = len(key_blocks)
    x_width = x.shape[1] // count
    heads = min(4, kv_width // DH) if count <= 4 else 1
    width = heads * DH
    x_steps = x_width // width
    assert x_width <= kv_width and x_width % width == 0
    wide = pl.BlockSpec((rows, group * width), lambda g, _: (0, g))
    narrow = pl.BlockSpec((rows, width), lambda g, _: (0, g))
    columns = [
        pl.BlockSpec(
            (rows, width),
            lambda g, ref, m=m: (0, (ref[0] ^ m) * x_steps + jnp.minimum(g, x_steps - 1)),
        )
        for m in range(1, count)
    ]
    out = pl.pallas_call(
        functools.partial(attention_kernel, count, group, heads, x_steps),
        grid_spec=pltpu.PrefetchScalarGridSpec(
            num_scalar_prefetch=1,
            grid=(kv_width // width,),
            in_specs=[wide, wide] + [narrow] * count + columns,
            out_specs=[narrow] * (2 * count - 1),
        ),
        out_shape=[jax.ShapeDtypeStruct((rows, kv_width), jnp.bfloat16)] * count
        + [pltpu.HBM((rows, kv_width), jnp.bfloat16)] * (count - 1),
        compiler_params=pltpu.CompilerParams(vmem_limit_bytes=(24 + 2 * count) * MIB),
    )(slot, *in_hbm(queries, grads, key_blocks[0]), *key_blocks[1:], *in_hbm(*[x] * (count - 1)))
    return out[:count], out[count:]


def rms_kernel(x_ref, out_ref):
    x = x_ref[...].astype(jnp.float32)
    inv_rms = lax.rsqrt(jnp.mean(x * x, axis=1, keepdims=True) + EPSILON)
    out_ref[...] = jnp.broadcast_to(inv_rms, out_ref.shape)


def inverse_rms(x):
    rows, width = x.shape
    step = min(rows, 2 * TILE)
    return pl.pallas_call(
        rms_kernel,
        grid=(rows // step,),
        in_specs=[pl.BlockSpec((step, width), lambda r: (r, 0))],
        out_specs=pl.BlockSpec((step, DH), lambda r: (r, 0)),
        out_shape=jax.ShapeDtypeStruct((rows, DH), jnp.float32),
        compiler_params=PARAMS,
    )(*in_hbm(x))


def value_kernel(count, slot_ref, rms_ref, own_ref, *refs):
    slot = slot_ref[0]
    total = own_ref[...].astype(jnp.float32)
    for m in range(1, count):
        total += jnp.where(slot ^ m > slot, refs[m - 1][...].astype(jnp.float32), 0.0)
        refs[count - 1 + m][...] = refs[m - 1][...]
    refs[count - 1][...] = (total * rms_ref[:, :1]).astype(jnp.bfloat16)


def value_grad(slot, inv_rms, own_term, received):
    rows, width = own_term.shape
    step = min(rows, 4 * TILE)
    count = len(received) + 1
    line = pl.BlockSpec((step, width), lambda r: (r, 0))
    out = pl.pallas_call(
        functools.partial(value_kernel, count),
        grid=(rows // step,),
        in_specs=[SCALAR, pl.BlockSpec((step, DH), lambda r: (r, 0))] + [line] * count,
        out_specs=[line] * count,
        out_shape=[jax.ShapeDtypeStruct((rows, width), jnp.bfloat16)]
        + [pltpu.HBM((rows, width), jnp.bfloat16)] * (count - 1),
        compiler_params=PARAMS,
    )(slot, inv_rms, own_term, *received)
    return out[0], out[1:]


def hold_kernel(*refs):
    count = len(refs) // 2
    for in_ref, out_ref in zip(refs[:count], refs[count:]):
        out_ref[...] = in_ref[...]


def held(*arrays):
    rows, width = arrays[0].shape
    step = min(rows, 2 * TILE)
    wide = [pl.BlockSpec((step, width), lambda r: (r, 0))] * len(arrays)
    return pl.pallas_call(
        hold_kernel,
        grid=(rows // step,),
        in_specs=wide,
        out_specs=wide,
        out_shape=[pltpu.HBM(array.shape, array.dtype) for array in arrays],
        compiler_params=PARAMS,
    )(*arrays)


def column_kernel(count, slot_ref, gain_ref, own_ref, *refs):
    first, second, out_ref = refs[: count - 1], refs[count - 1 : -1], refs[-1]
    slot = slot_ref[0]
    rows = own_ref.shape[0]
    gain = gain_ref[...].astype(jnp.float32)
    for m in range(count):
        x = own_ref[...]
        if m > 0:
            x = jnp.where(slot ^ m > slot, first[m - 1][...], second[m - 1][...])
        out_ref[:, m * rows : (m + 1) * rows] = (x.astype(jnp.float32) * gain).astype(jnp.bfloat16).T


def gained_columns(slot, gain, x, first, second):
    count = len(first) + 1
    rows, width = x.shape
    width = width // count
    step = min(width, 256)
    steps = width // step
    column = pl.BlockSpec((rows, step), lambda c, _: (0, c))
    return pl.pallas_call(
        functools.partial(column_kernel, count),
        grid_spec=pltpu.PrefetchScalarGridSpec(
            num_scalar_prefetch=1,
            grid=(steps,),
            in_specs=[
                pl.BlockSpec((1, step), lambda c, _: (0, c)),
                pl.BlockSpec((rows, step), lambda c, slot_ref: (0, slot_ref[0] * steps + c)),
            ]
            + [column] * (2 * count - 2),
            out_specs=pl.BlockSpec((step, count * rows), lambda c, _: (c, 0)),
        ),
        out_shape=jax.ShapeDtypeStruct((width, count * rows), jnp.bfloat16),
        compiler_params=PARAMS,
    )(slot, *in_hbm(gain, x), *first, *second)


def feature_kernel(count, weight_ref, gain_ref, *refs):
    value_refs, scaled_refs = refs[:count], refs[count:]
    rows = value_refs[0].shape[0]
    values = jnp.concatenate([ref[...] for ref in value_refs], axis=0)
    normed_grad = lax.dot_general(
        values, weight_ref[...], (((1,), (1,)), ((), ())), preferred_element_type=jnp.float32
    )
    gain = gain_ref[...].astype(jnp.float32)
    for m in range(count):
        scaled_refs[m][...] = (normed_grad[m * rows : (m + 1) * rows] * gain).astype(jnp.bfloat16)


def feature_grads(weight, gain, values):
    count = len(values)
    rows, kv_width = values[0].shape
    width = weight.shape[0]
    step = min(width, 1024)
    column = pl.BlockSpec((rows, step), lambda c: (0, c))
    return pl.pallas_call(
        functools.partial(feature_kernel, count),
        grid=(width // step,),
        in_specs=[
            pl.BlockSpec((step, kv_width), lambda c: (c, 0)),
            pl.BlockSpec((1, step), lambda c: (0, c)),
        ]
        + [fixed((rows, kv_width))] * count,
        out_specs=[column] * count,
        out_shape=[jax.ShapeDtypeStruct((rows, width), jnp.bfloat16)] * count,
        compiler_params=PARAMS,
    )(weight, *in_hbm(gain), *values)


def weight_product(weight_ref, gain_ref, columns_ref, value_refs):
    values = jnp.concatenate([ref[...] for ref in value_refs], axis=0)
    grad = jnp.dot(columns_ref[...], values, preferred_element_type=jnp.float32)
    terms = grad * weight_ref[...].astype(jnp.float32)
    lanes = sum(terms[:, i : i + DH] for i in range(0, grad.shape[1], DH))
    line = jnp.sum(lanes.T, axis=0, keepdims=True) / gain_ref[...].astype(jnp.float32)
    return grad, line


def sent_kernel(half_ref, weight_ref, gain_ref, columns_ref, *refs):
    out_ref = refs[-1]
    grad, line = weight_product(weight_ref, gain_ref, columns_ref, refs[:-1])
    width, kv_width = grad.shape
    out_ref[:width, :] = grad.astype(jnp.bfloat16)
    out_ref[width:, :] = jnp.zeros((TILE, kv_width), jnp.bfloat16)
    out_ref[width:, :width] = jnp.broadcast_to(line, (TILE, width)).astype(jnp.bfloat16)


def kept_kernel(half_ref, weight_ref, gain_ref, columns_ref, got_ref, *refs):
    out_ref, line_ref = refs[-2:]
    grad, line = weight_product(weight_ref, gain_ref, columns_ref, refs[:-2])
    width = grad.shape[0]
    out_ref[...] = (grad + got_ref[:width, :].astype(jnp.float32)).astype(jnp.bfloat16)
    line_ref[...] = line + got_ref[width:, :width].astype(jnp.float32)[:1]


def weight_grad(half, halves, weight, gain, columns, values, got=None):
    rows, kv_width = values[0].shape
    width, tokens = columns.shape
    width = width // halves
    message = (width + TILE, kv_width)
    if got is None:
        kernel, extra = sent_kernel, []
        out_specs, out_shape = fixed(message), jax.ShapeDtypeStruct(message, jnp.bfloat16)
    else:
        kernel, extra = kept_kernel, [got]
        out_specs = [fixed((width, kv_width)), fixed((1, width))]
        out_shape = [
            jax.ShapeDtypeStruct((width, kv_width), jnp.bfloat16),
            jax.ShapeDtypeStruct((1, width), jnp.float32),
        ]
    return pl.pallas_call(
        kernel,
        grid_spec=pltpu.PrefetchScalarGridSpec(
            num_scalar_prefetch=1,
            grid=(1,),
            in_specs=[
                pl.BlockSpec((width, kv_width), lambda c, half_ref: (half_ref[0], 0)),
                pl.BlockSpec((1, width), lambda c, half_ref: (0, half_ref[0])),
                pl.BlockSpec((width, tokens), lambda c, half_ref: (half_ref[0], 0)),
            ]
            + [fixed(message)] * len(extra)
            + [fixed((rows, kv_width))] * len(values),
            out_specs=out_specs,
        ),
        out_shape=out_shape,
        compiler_params=PARAMS,
    )(half, weight, *in_hbm(gain), columns, *extra, *values)


def stage_kernel(in_ref, out_ref):
    pltpu.sync_copy(in_ref, out_ref)


def staged(array):
    return pl.pallas_call(
        stage_kernel,
        in_specs=[pl.BlockSpec(memory_space=pltpu.HBM)],
        out_specs=pl.BlockSpec(memory_space=pltpu.VMEM),
        out_shape=pltpu.VMEM(array.shape, array.dtype),
        compiler_params=PARAMS,
    )(array)


def input_kernel(count, slot_ref, x_ref, grad_ref, *refs):
    scaled_refs, out_ref = [refs[count - 1], refs[count - 2], *refs[: count - 2]], refs[count]
    slot = slot_ref[0]
    x = x_ref[...].astype(jnp.float32)
    square = 1.0 / (jnp.mean(x * x, axis=1, keepdims=True) + EPSILON)
    width = x.shape[1] // count
    starts = [pl.multiple_of((slot ^ m) * width, width) for m in range(count)]
    inner = jnp.zeros_like(square)
    for m in range(count):
        block = x_ref[:, pl.ds(starts[m], width)].astype(jnp.float32)
        inner += jnp.sum(scaled_refs[m][...].astype(jnp.float32) * block, axis=1, keepdims=True)
    inner = inner * square / x.shape[1]
    for m in range(count):
        columns = pl.ds(starts[m], width)
        block = x_ref[:, columns].astype(jnp.float32)
        grad = grad_ref[:, columns].astype(jnp.float32)
        scaled = scaled_refs[m][...].astype(jnp.float32)
        out_ref[:, columns] = (grad + (scaled - block * inner)).astype(jnp.bfloat16)


def input_grad(slot, x, grads, scaled):
    count = len(scaled)
    rows, width = x.shape
    step = min(rows, 4 * TILE)
    wide = pl.BlockSpec((step, width), lambda r: (r, 0))
    return pl.pallas_call(
        functools.partial(input_kernel, count),
        grid=(rows // step,),
        in_specs=[SCALAR, wide, wide]
        + [pl.BlockSpec((step, width // count), lambda r: (r, 0))] * count,
        out_specs=wide,
        out_shape=jax.ShapeDtypeStruct((rows, width), jnp.bfloat16),
        compiler_params=PARAMS,
    )(slot, x, grads, *scaled[2:], *scaled[1::-1])


def per_device(section_inputs, queries, keys, w_value, gain, section_grads_in):
    count = lax.axis_size("fsdp")
    docs = lax.axis_size("dp")
    slot = lax.axis_index("fsdp").astype(jnp.int32)[None]
    half = lax.axis_index("dp").astype(jnp.int32)[None]
    x, cotangent, own_keys = section_inputs[0, 0], section_grads_in[0, 0], keys[0, 0]
    weight = w_value[0]
    assert MEM <= x.shape[0] and docs == 2 and count & (count - 1) == 0
    masks = range(1, count)
    turns = [*masks[1:], 1]

    swap = [(0, 1), (1, 0)]

    x_width = x.shape[1] // count
    first = []
    for m in masks:
        columns = lax.dynamic_slice_in_dim(x, (slot[0] ^ m) * x_width, x_width, axis=1)
        columns = jnp.pad(columns, ((0, 0), (0, own_keys.shape[1] - x_width)))
        first.append(to_partner(jnp.where(slot[0] ^ m > slot[0], own_keys, columns), m))
    next_x = lax.ppermute(x, "section", section_route(-1))
    next_grad = lax.ppermute(cotangent, "section", section_route(-1))
    inv_rms = inverse_rms(x)
    first, inv_rms, slot = after((first, inv_rms, slot), ())
    terms, first = attention(slot, queries[0, 0], cotangent, [own_keys] + first, x)

    second = [to_partner(terms[m], m) for m in reversed(masks)][::-1]
    next_x, next_grad = held(next_x, next_grad)
    second, next_x, next_grad = after(([second[m - 1] for m in turns], next_x, next_grad), ())
    second = [second[turns.index(m)] for m in masks]
    value, second = value_grad(slot, inv_rms, terms[0], second)

    values = [value] + [to_partner(value, m) for m in masks]
    columns = gained_columns(slot, gain, x, first, second)
    weight = staged(weight)
    others, columns, weight = after(([values[m] for m in turns], columns, weight), ())
    values = [value] + [others[turns.index(m)] for m in masks]

    sent = weight_grad(1 - half, docs, weight, gain, columns, values)
    scaled = feature_grads(weight, gain, values)
    returned = [to_partner(scaled[m], m, below=True) for m in range(count)]
    got = lax.ppermute(sent, "dp", swap)
    weight_out, gain_out = weight_grad(half, docs, weight, gain, columns, values, got)
    slot = after(slot, weight_out)
    passed = input_grad(slot, next_x, next_grad, returned)
    return passed[None, None], weight_out[None], gain_out


def solution(mesh):
    return jax.shard_map(
        per_device,
        mesh=mesh,
        in_specs=(
            P("section", "dp", "fsdp", None),
            P("section", "dp", "fsdp", None),
            P("section", "dp", "fsdp", None),
            P("section", "fsdp", None),
            P("section", "fsdp"),
            P("section", "dp", "fsdp", None),
        ),
        out_specs=(
            P("section", "dp", "fsdp", None),
            P("section", ("fsdp", "dp"), None),
            P("section", ("fsdp", "dp")),
        ),
        check_vma=False,
    )
```

```python
import functools

import jax
import jax.numpy as jnp
from jax import lax
from jax.experimental import pallas as pl
from jax.experimental.pallas import tpu as pltpu
from jax.sharding import PartitionSpec as P

DH = 128
MEM = 128
NEG_FILL = -1e30
EPSILON = 1e-05
LOG2E = 1.4426950408889634
TILE = 16
MIB = 1024 * 1024

SCALAR = pl.BlockSpec(memory_space=pltpu.SMEM)
IN_VMEM = pl.BlockSpec(memory_space=pltpu.VMEM)
IN_HBM = pl.BlockSpec(memory_space=pltpu.HBM)
PARAMS = pltpu.CompilerParams(vmem_limit_bytes=16 * MIB)


def section_route(distance):
    count = lax.axis_size("section")
    return [(s, (s + distance) % count) for s in range(count)]


def to_partner(block, mask, below=False):
    sections, count = lax.axis_size("section"), lax.axis_size("fsdp")
    route = [
        (s * count + f, (s - below) % sections * count + (f ^ mask))
        for s in range(sections)
        for f in range(count)
    ]
    return lax.ppermute(block, ("section", "fsdp"), route)


def after(arrays, others):
    kept, _ = lax.optimization_barrier((arrays, others))
    return kept


def fixed(shape):
    return pl.BlockSpec(shape, lambda *_: (0, 0))


def in_hbm(*arrays):
    return [pltpu.with_memory_space_constraint(array, pltpu.HBM) for array in arrays]


def started(refs, others, sems):
    copies = [
        pltpu.make_async_copy(ref, other, sems.at[i])
        for i, (ref, other) in enumerate(zip(refs, others))
    ]
    for copy in copies:
        copy.start()
    return copies


def attention_kernel(count, group, heads, slot_ref, query_ref, grad_ref, *refs):
    key_refs, x_refs = refs[:count], refs[count : 2 * count - 1]
    out_refs, kept_refs = refs[2 * count - 1 : 3 * count - 1], refs[3 * count - 1 : -1]
    copies = started(key_refs[1:], kept_refs, refs[-1])
    rows, kv_width = key_refs[0].shape
    slot = slot_ref[0]
    key_at = lax.broadcasted_iota(jnp.int32, (rows, rows), 0)
    query_at = lax.broadcasted_iota(jnp.int32, (rows, rows), 1)
    visible = (key_at <= query_at) | (slot * rows + key_at < MEM)
    visible = jnp.concatenate([visible] * group, axis=1)
    hidden = [0.0] + [jnp.where(slot ^ m < slot, 0.0, NEG_FILL) for m in range(1, count)]
    scale = DH ** (-0.5) * LOG2E

    def head_values(head):
        own = pl.ds(pl.multiple_of(head * DH, DH), DH)
        members = [
            pl.ds(pl.multiple_of((head * group + h) * DH, DH), DH) for h in range(group)
        ]
        query = jnp.concatenate([query_ref[:, h] for h in members], axis=0)
        grad = jnp.concatenate([grad_ref[:, h] for h in members], axis=0)
        keys = jnp.concatenate([ref[:, own] for ref in key_refs], axis=0)
        scores = lax.dot_general(
            keys, query, (((1,), (1,)), ((), ())), preferred_element_type=jnp.float32
        )
        parts = [scores[m * rows : (m + 1) * rows] for m in range(count)]
        parts[0] = jnp.where(visible, parts[0], NEG_FILL)
        tops = [jnp.max(part, axis=0, keepdims=True) + hide for part, hide in zip(parts, hidden)]
        top = functools.reduce(jnp.maximum, tops)
        weights = [jnp.exp2((part - (top - hide)) * scale) for part, hide in zip(parts, hidden)]
        sums = [jnp.sum(weight, axis=0, keepdims=True) for weight in weights]
        inverse = 1.0 / functools.reduce(jnp.add, sums)
        probs = jnp.concatenate([(w * inverse).astype(jnp.bfloat16) for w in weights], axis=0)
        values = jnp.dot(probs, grad, preferred_element_type=jnp.float32)
        for m in range(count):
            out_refs[m][:, own] = values[m * rows : (m + 1) * rows].astype(jnp.bfloat16)

    @pl.loop(0, kv_width // DH // heads)
    def _(step):
        for head in range(heads):
            head_values(step * heads + head)

    for m in range(1, count):

        @pl.when(slot ^ m > slot)
        def _():
            out_refs[m][:, : x_refs[m - 1].shape[1]] = x_refs[m - 1][...]

    for copy in copies:
        copy.wait()


def attention(slot, queries, grads, key_blocks, x_blocks):
    rows, kv_width = key_blocks[0].shape
    group = queries.shape[1] // kv_width
    count = len(key_blocks)
    heads = min(4, kv_width // DH) if count <= 4 else 1
    assert x_blocks[0].shape[1] <= kv_width
    block = (rows, kv_width)
    out = pl.pallas_call(
        functools.partial(attention_kernel, count, group, heads),
        in_specs=[SCALAR] + [IN_VMEM] * (2 * count + 1),
        out_specs=[IN_VMEM] * count + [IN_HBM] * (count - 1),
        out_shape=[pltpu.VMEM(block, jnp.bfloat16)] * count
        + [pltpu.HBM(block, jnp.bfloat16)] * (count - 1),
        scratch_shapes=[pltpu.SemaphoreType.DMA((count - 1,))],
        compiler_params=pltpu.CompilerParams(vmem_limit_bytes=(12 + 2 * count) * MIB),
    )(slot, queries, grads, *key_blocks, *x_blocks)
    return out[:count], out[count:]


def prepare_kernel(count, slot_ref, x_ref, rms_ref, *out_refs):
    x = x_ref[...].astype(jnp.float32)
    inv_rms = lax.rsqrt(jnp.mean(x * x, axis=1, keepdims=True) + EPSILON)
    rms_ref[...] = jnp.broadcast_to(inv_rms, rms_ref.shape)
    width = x.shape[1] // count
    for m in range(1, count):
        start = pl.multiple_of((slot_ref[0] ^ m) * width, width)
        out_refs[m - 1][...] = x_ref[:, pl.ds(start, width)]


def prepared(slot, x, count):
    rows, width = x.shape
    step = min(rows, 2 * TILE)
    block = (rows, width // count)
    out = pl.pallas_call(
        functools.partial(prepare_kernel, count),
        grid=(rows // step,),
        in_specs=[SCALAR, pl.BlockSpec((step, width), lambda r: (r, 0))],
        out_specs=[pl.BlockSpec((step, DH), lambda r: (r, 0))]
        + [pl.BlockSpec((step, width // count), lambda r: (r, 0))] * (count - 1),
        out_shape=[pltpu.VMEM((rows, DH), jnp.float32)]
        + [pltpu.VMEM(block, jnp.bfloat16)] * (count - 1),
        compiler_params=PARAMS,
    )(slot, *in_hbm(x))
    return out[0], out[1:]


def value_kernel(count, slot_ref, rms_ref, own_ref, *refs):
    received, out_ref, kept_refs = refs[: count - 1], refs[count - 1], refs[count:-1]
    copies = started(received, kept_refs, refs[-1])
    slot = slot_ref[0]
    total = own_ref[...].astype(jnp.float32)
    for m in range(1, count):
        total += jnp.where(slot ^ m > slot, received[m - 1][...].astype(jnp.float32), 0.0)
    out_ref[...] = (total * rms_ref[:, :1]).astype(jnp.bfloat16)
    for copy in copies:
        copy.wait()


def value_grad(slot, inv_rms, own_term, received):
    block = own_term.shape
    count = len(received) + 1
    out = pl.pallas_call(
        functools.partial(value_kernel, count),
        in_specs=[SCALAR] + [IN_VMEM] * (count + 1),
        out_specs=[IN_VMEM] + [IN_HBM] * (count - 1),
        out_shape=[pltpu.VMEM(block, jnp.bfloat16)]
        + [pltpu.HBM(block, jnp.bfloat16)] * (count - 1),
        scratch_shapes=[pltpu.SemaphoreType.DMA((count - 1,))],
        compiler_params=PARAMS,
    )(slot, inv_rms, own_term, *received)
    return out[0], out[1:]


def hold_kernel(*refs):
    count = len(refs) // 2
    for in_ref, out_ref in zip(refs[:count], refs[count:]):
        out_ref[...] = in_ref[...]


def held(*arrays):
    rows, width = arrays[0].shape
    step = min(rows, 2 * TILE)
    wide = [pl.BlockSpec((step, width), lambda r: (r, 0))] * len(arrays)
    return pl.pallas_call(
        hold_kernel,
        grid=(rows // step,),
        in_specs=wide,
        out_specs=wide,
        out_shape=[pltpu.HBM(array.shape, array.dtype) for array in arrays],
        compiler_params=PARAMS,
    )(*arrays)


def column_kernel(count, slot_ref, gain_ref, own_ref, *refs):
    first, second, out_ref = refs[: count - 1], refs[count - 1 : -1], refs[-1]
    slot = slot_ref[0]
    rows = own_ref.shape[0]
    gain = gain_ref[...].astype(jnp.float32)
    for m in range(count):
        x = own_ref[...]
        if m > 0:
            x = jnp.where(slot ^ m > slot, first[m - 1][...], second[m - 1][...])
        out_ref[:, m * rows : (m + 1) * rows] = (x.astype(jnp.float32) * gain).astype(jnp.bfloat16).T


def gained_columns(slot, gain, x, first, second):
    count = len(first) + 1
    rows, width = x.shape
    width = width // count
    step = min(width, 256)
    steps = width // step
    column = pl.BlockSpec((rows, step), lambda c, _: (0, c))
    return pl.pallas_call(
        functools.partial(column_kernel, count),
        grid_spec=pltpu.PrefetchScalarGridSpec(
            num_scalar_prefetch=1,
            grid=(steps,),
            in_specs=[
                pl.BlockSpec((1, step), lambda c, _: (0, c)),
                pl.BlockSpec((rows, step), lambda c, slot_ref: (0, slot_ref[0] * steps + c)),
            ]
            + [column] * (2 * count - 2),
            out_specs=pl.BlockSpec((step, count * rows), lambda c, _: (c, 0)),
        ),
        out_shape=pltpu.VMEM((width, count * rows), jnp.bfloat16),
        compiler_params=PARAMS,
    )(slot, *in_hbm(gain, x), *first, *second)


def feature_kernel(count, weight_ref, gain_ref, *refs):
    value_refs, scaled_refs = refs[:count], refs[count:]
    rows = value_refs[0].shape[0]
    values = jnp.concatenate([ref[...] for ref in value_refs], axis=0)
    normed_grad = lax.dot_general(
        values, weight_ref[...], (((1,), (1,)), ((), ())), preferred_element_type=jnp.float32
    )
    gain = gain_ref[...].astype(jnp.float32)
    for m in range(count):
        scaled_refs[m][...] = (normed_grad[m * rows : (m + 1) * rows] * gain).astype(jnp.bfloat16)


def feature_grads(weight, gain, values):
    count = len(values)
    block = (values[0].shape[0], weight.shape[0])
    return pl.pallas_call(
        functools.partial(feature_kernel, count),
        in_specs=[IN_VMEM] * (count + 2),
        out_specs=[IN_VMEM] * count,
        out_shape=[pltpu.VMEM(block, jnp.bfloat16)] * count,
        compiler_params=PARAMS,
    )(weight, gain, *values)


def weight_product(half, width, weight_ref, gain_ref, columns_ref, value_refs):
    values = jnp.concatenate([ref[...] for ref in value_refs], axis=0)
    start = pl.multiple_of(half * width, width)
    lines = pl.ds(start, width)
    grad = jnp.dot(columns_ref[lines, :], values, preferred_element_type=jnp.float32)
    terms = grad * weight_ref[lines, :].astype(jnp.float32)
    lanes = sum(terms[:, i : i + DH] for i in range(0, grad.shape[1], DH))
    line = jnp.sum(lanes.T, axis=0, keepdims=True) / gain_ref[:, lines].astype(jnp.float32)
    return grad, line


def sent_kernel(half_ref, weight_ref, gain_ref, columns_ref, *refs):
    out_ref = refs[-1]
    width, kv_width = out_ref.shape[0] - TILE, out_ref.shape[1]
    grad, line = weight_product(half_ref[0], width, weight_ref, gain_ref, columns_ref, refs[:-1])
    out_ref[:width, :] = grad.astype(jnp.bfloat16)
    out_ref[width:, :] = jnp.zeros((TILE, kv_width), jnp.bfloat16)
    out_ref[width:, :width] = jnp.broadcast_to(line, (TILE, width)).astype(jnp.bfloat16)


def kept_kernel(half_ref, weight_ref, gain_ref, columns_ref, got_ref, *refs):
    out_ref, line_ref = refs[-2:]
    width = out_ref.shape[0]
    grad, line = weight_product(half_ref[0], width, weight_ref, gain_ref, columns_ref, refs[:-2])
    out_ref[...] = (grad + got_ref[:width, :].astype(jnp.float32)).astype(jnp.bfloat16)
    line_ref[...] = line + got_ref[width:, :width].astype(jnp.float32)[:1]


def weight_grad(half, halves, weight, gain, columns, values, got=None):
    kv_width = values[0].shape[1]
    width = columns.shape[0] // halves
    message = (width + TILE, kv_width)
    if got is None:
        kernel, extra = sent_kernel, []
        out_specs, out_shape = IN_VMEM, pltpu.VMEM(message, jnp.bfloat16)
    else:
        kernel, extra = kept_kernel, [got]
        out_specs = [fixed((width, kv_width)), fixed((1, width))]
        out_shape = [
            jax.ShapeDtypeStruct((width, kv_width), jnp.bfloat16),
            jax.ShapeDtypeStruct((1, width), jnp.float32),
        ]
    return pl.pallas_call(
        kernel,
        grid=(1,),
        in_specs=[SCALAR] + [IN_VMEM] * (3 + len(extra) + len(values)),
        out_specs=out_specs,
        out_shape=out_shape,
        compiler_params=PARAMS,
    )(half, weight, gain, columns, *extra, *values)


def stage_kernel(in_ref, out_ref):
    pltpu.sync_copy(in_ref, out_ref)


def staged(array):
    return pl.pallas_call(
        stage_kernel,
        in_specs=[IN_HBM],
        out_specs=IN_VMEM,
        out_shape=pltpu.VMEM(array.shape, array.dtype),
        compiler_params=PARAMS,
    )(array)


def input_kernel(count, slot_ref, x_ref, grad_ref, *refs):
    scaled_refs, out_ref = [refs[count - 1], refs[count - 2], *refs[: count - 2]], refs[count]
    slot = slot_ref[0]
    x = x_ref[...].astype(jnp.float32)
    square = 1.0 / (jnp.mean(x * x, axis=1, keepdims=True) + EPSILON)
    width = x.shape[1] // count
    starts = [pl.multiple_of((slot ^ m) * width, width) for m in range(count)]
    inner = jnp.zeros_like(square)
    for m in range(count):
        block = x_ref[:, pl.ds(starts[m], width)].astype(jnp.float32)
        inner += jnp.sum(scaled_refs[m][...].astype(jnp.float32) * block, axis=1, keepdims=True)
    inner = inner * square / x.shape[1]
    for m in range(count):
        columns = pl.ds(starts[m], width)
        block = x_ref[:, columns].astype(jnp.float32)
        grad = grad_ref[:, columns].astype(jnp.float32)
        scaled = scaled_refs[m][...].astype(jnp.float32)
        out_ref[:, columns] = (grad + (scaled - block * inner)).astype(jnp.bfloat16)


def input_grad(slot, x, grads, scaled):
    count = len(scaled)
    rows, width = x.shape
    step = min(rows, 4 * TILE)
    wide = pl.BlockSpec((step, width), lambda r: (r, 0))
    return pl.pallas_call(
        functools.partial(input_kernel, count),
        grid=(rows // step,),
        in_specs=[SCALAR, wide, wide]
        + [pl.BlockSpec((step, width // count), lambda r: (r, 0))] * count,
        out_specs=wide,
        out_shape=jax.ShapeDtypeStruct((rows, width), jnp.bfloat16),
        compiler_params=PARAMS,
    )(slot, x, grads, *scaled[2:], *scaled[1::-1])


def per_device(section_inputs, queries, keys, w_value, gain, section_grads_in):
    count = lax.axis_size("fsdp")
    docs = lax.axis_size("dp")
    slot = lax.axis_index("fsdp").astype(jnp.int32)[None]
    half = lax.axis_index("dp").astype(jnp.int32)[None]
    x, cotangent, own_keys = section_inputs[0, 0], section_grads_in[0, 0], keys[0, 0]
    weight = w_value[0]
    assert MEM <= x.shape[0] and docs == 2 and count & (count - 1) == 0
    masks = range(1, count)
    turns = [*masks[1:], 1]

    swap = [(0, 1), (1, 0)]

    x_width = x.shape[1] // count
    first = []
    for m in masks:
        columns = lax.dynamic_slice_in_dim(x, (slot[0] ^ m) * x_width, x_width, axis=1)
        columns = jnp.pad(columns, ((0, 0), (0, own_keys.shape[1] - x_width)))
        first.append(to_partner(jnp.where(slot[0] ^ m > slot[0], own_keys, columns), m))
    next_x = lax.ppermute(x, "section", section_route(-1))
    next_grad = lax.ppermute(cotangent, "section", section_route(-1))
    inv_rms, x_blocks = prepared(slot, x, count)
    query, grad, held_keys = staged(queries[0, 0]), staged(cotangent), staged(own_keys)
    first, inv_rms, x_blocks, query, grad, held_keys = after(
        (first, inv_rms, x_blocks, query, grad, held_keys), ()
    )
    terms, first = attention(slot, query, grad, [held_keys] + first, x_blocks)

    second = [to_partner(terms[m], m) for m in reversed(masks)][::-1]
    next_x, next_grad = held(next_x, next_grad)
    second, next_x, next_grad = after(([second[m - 1] for m in turns], next_x, next_grad), ())
    second = [second[turns.index(m)] for m in masks]
    value, second = value_grad(slot, inv_rms, terms[0], second)

    values = [value] + [to_partner(value, m) for m in masks]
    columns = gained_columns(slot, gain, x, first, second)
    weight, held_gain = staged(weight), staged(gain)
    others, columns, weight, held_gain = after(
        ([values[m] for m in turns], columns, weight, held_gain), ()
    )
    values = [value] + [others[turns.index(m)] for m in masks]

    sent = weight_grad(1 - half, docs, weight, held_gain, columns, values)
    scaled = feature_grads(weight, held_gain, values)
    returned = [to_partner(scaled[m], m, below=True) for m in range(count)]
    got = lax.ppermute(sent, "dp", swap)
    weight_out, gain_out = weight_grad(half, docs, weight, held_gain, columns, values, got)
    slot = after(slot, weight_out)
    passed = input_grad(slot, next_x, next_grad, returned)
    return passed[None, None], weight_out[None], gain_out


def solution(mesh):
    return jax.shard_map(
        per_device,
        mesh=mesh,
        in_specs=(
            P("section", "dp", "fsdp", None),
            P("section", "dp", "fsdp", None),
            P("section", "dp", "fsdp", None),
            P("section", "fsdp", None),
            P("section", "fsdp"),
            P("section", "dp", "fsdp", None),
        ),
        out_specs=(
            P("section", "dp", "fsdp", None),
            P("section", ("fsdp", "dp"), None),
            P("section", ("fsdp", "dp")),
        ),
        check_vma=False,
    )
```

```python
import functools

import jax
import jax.numpy as jnp
from jax import lax
from jax.experimental import pallas as pl
from jax.experimental.pallas import tpu as pltpu
from jax.sharding import PartitionSpec as P

DH = 128
MEM = 128
NEG_FILL = -1e30
EPSILON = 1e-05
LOG2E = 1.4426950408889634
TILE = 16
MIB = 1024 * 1024

SCALAR = pl.BlockSpec(memory_space=pltpu.SMEM)
IN_VMEM = pl.BlockSpec(memory_space=pltpu.VMEM)
IN_HBM = pl.BlockSpec(memory_space=pltpu.HBM)
PARAMS = pltpu.CompilerParams(vmem_limit_bytes=16 * MIB)


def section_route(distance):
    count = lax.axis_size("section")
    return [(s, (s + distance) % count) for s in range(count)]


def to_partner(block, mask, below=False):
    sections, count = lax.axis_size("section"), lax.axis_size("fsdp")
    route = [
        (s * count + f, (s - below) % sections * count + (f ^ mask))
        for s in range(sections)
        for f in range(count)
    ]
    return lax.ppermute(block, ("section", "fsdp"), route)


def after(arrays, others):
    kept, _ = lax.optimization_barrier((arrays, others))
    return kept


def fixed(shape):
    return pl.BlockSpec(shape, lambda *_: (0, 0))


def in_hbm(*arrays):
    return [pltpu.with_memory_space_constraint(array, pltpu.HBM) for array in arrays]


def started(refs, others, sems):
    copies = [
        pltpu.make_async_copy(ref, other, sems.at[i])
        for i, (ref, other) in enumerate(zip(refs, others))
    ]
    for copy in copies:
        copy.start()
    return copies


def attention_kernel(count, group, heads, slot_ref, query_ref, grad_ref, *refs):
    key_refs, x_refs = refs[:count], refs[count : 2 * count - 1]
    out_refs, kept_refs = refs[2 * count - 1 : 3 * count - 1], refs[3 * count - 1 : -1]
    copies = started(key_refs[1:], kept_refs, refs[-1])
    rows, kv_width = key_refs[0].shape
    slot = slot_ref[0]
    key_at = lax.broadcasted_iota(jnp.int32, (rows, rows), 0)
    query_at = lax.broadcasted_iota(jnp.int32, (rows, rows), 1)
    visible = (key_at <= query_at) | (slot * rows + key_at < MEM)
    visible = jnp.concatenate([visible] * group, axis=1)
    hidden = [0.0] + [jnp.where(slot ^ m < slot, 0.0, NEG_FILL) for m in range(1, count)]
    scale = DH ** (-0.5) * LOG2E

    def head_values(head):
        own = pl.ds(pl.multiple_of(head * DH, DH), DH)
        members = [
            pl.ds(pl.multiple_of((head * group + h) * DH, DH), DH) for h in range(group)
        ]
        query = jnp.concatenate([query_ref[:, h] for h in members], axis=0)
        grad = jnp.concatenate([grad_ref[:, h] for h in members], axis=0)
        keys = jnp.concatenate([ref[:, own] for ref in key_refs], axis=0)
        scores = lax.dot_general(
            keys, query, (((1,), (1,)), ((), ())), preferred_element_type=jnp.float32
        )
        parts = [scores[m * rows : (m + 1) * rows] for m in range(count)]
        parts[0] = jnp.where(visible, parts[0], NEG_FILL)
        tops = [jnp.max(part, axis=0, keepdims=True) + hide for part, hide in zip(parts, hidden)]
        top = functools.reduce(jnp.maximum, tops)
        weights = [jnp.exp2((part - (top - hide)) * scale) for part, hide in zip(parts, hidden)]
        sums = [jnp.sum(weight, axis=0, keepdims=True) for weight in weights]
        inverse = 1.0 / functools.reduce(jnp.add, sums)
        probs = jnp.concatenate([(w * inverse).astype(jnp.bfloat16) for w in weights], axis=0)
        values = jnp.dot(probs, grad, preferred_element_type=jnp.float32)
        for m in range(count):
            out_refs[m][:, own] = values[m * rows : (m + 1) * rows].astype(jnp.bfloat16)

    @pl.loop(0, kv_width // DH // heads)
    def _(step):
        for head in range(heads):
            head_values(step * heads + head)

    for m in range(1, count):

        @pl.when(slot ^ m > slot)
        def _():
            out_refs[m][:, : x_refs[m - 1].shape[1]] = x_refs[m - 1][...]

    for copy in copies:
        copy.wait()


def attention(slot, queries, grads, key_blocks, x_blocks):
    rows, kv_width = key_blocks[0].shape
    group = queries.shape[1] // kv_width
    count = len(key_blocks)
    heads = min(4, kv_width // DH) if count <= 4 else 1
    assert x_blocks[0].shape[1] <= kv_width
    block = (rows, kv_width)
    out = pl.pallas_call(
        functools.partial(attention_kernel, count, group, heads),
        in_specs=[SCALAR] + [IN_VMEM] * (2 * count + 1),
        out_specs=[IN_VMEM] * count + [IN_HBM] * (count - 1),
        out_shape=[pltpu.VMEM(block, jnp.bfloat16)] * count
        + [pltpu.HBM(block, jnp.bfloat16)] * (count - 1),
        scratch_shapes=[pltpu.SemaphoreType.DMA((count - 1,))],
        compiler_params=pltpu.CompilerParams(vmem_limit_bytes=(12 + 2 * count) * MIB),
    )(slot, queries, grads, *key_blocks, *x_blocks)
    return out[:count], out[count:]


def first_kernel(count, slot_ref, keys_ref, x_ref, *refs):
    out_refs, sems = refs[:-1], refs[-1]
    slot = slot_ref[0]
    width = x_ref.shape[1] // count
    for m in range(1, count):
        out_ref = out_refs[m - 1]
        columns = pl.ds(pl.multiple_of((slot ^ m) * width, width), width)

        @pl.when(slot ^ m > slot)
        def _():
            pltpu.make_async_copy(keys_ref, out_ref, sems.at[m - 1]).start()

        @pl.when(slot ^ m < slot)
        def _():
            if width < out_ref.shape[1]:
                out_ref[:, width:] = jnp.zeros_like(out_ref[:, width:])
            pltpu.make_async_copy(
                x_ref.at[:, columns], out_ref.at[:, :width], sems.at[m - 1]
            ).start()

    for m in range(1, count):
        out_ref = out_refs[m - 1]

        @pl.when(slot ^ m > slot)
        def _():
            pltpu.make_async_copy(keys_ref, out_ref, sems.at[m - 1]).wait()

        @pl.when(slot ^ m < slot)
        def _():
            pltpu.make_async_copy(
                x_ref.at[:, :width], out_ref.at[:, :width], sems.at[m - 1]
            ).wait()


def first_blocks(slot, keys, x, count):
    return pl.pallas_call(
        functools.partial(first_kernel, count),
        in_specs=[SCALAR, IN_HBM, IN_HBM],
        out_specs=[IN_VMEM] * (count - 1),
        out_shape=[pltpu.VMEM(keys.shape, keys.dtype)] * (count - 1),
        scratch_shapes=[pltpu.SemaphoreType.DMA((count - 1,))],
        compiler_params=PARAMS,
    )(slot, *in_hbm(keys, x))


def prepare_kernel(count, slot_ref, x_ref, rms_ref, *out_refs):
    x = x_ref[...].astype(jnp.float32)
    inv_rms = lax.rsqrt(jnp.mean(x * x, axis=1, keepdims=True) + EPSILON)
    rms_ref[...] = jnp.broadcast_to(inv_rms, rms_ref.shape)
    width = x.shape[1] // count
    for m in range(1, count):
        start = pl.multiple_of((slot_ref[0] ^ m) * width, width)
        out_refs[m - 1][...] = x_ref[:, pl.ds(start, width)]


def prepared(slot, x, count):
    rows, width = x.shape
    step = min(rows, 2 * TILE)
    block = (rows, width // count)
    out = pl.pallas_call(
        functools.partial(prepare_kernel, count),
        grid=(rows // step,),
        in_specs=[SCALAR, pl.BlockSpec((step, width), lambda r: (r, 0))],
        out_specs=[pl.BlockSpec((step, DH), lambda r: (r, 0))]
        + [pl.BlockSpec((step, width // count), lambda r: (r, 0))] * (count - 1),
        out_shape=[pltpu.VMEM((rows, DH), jnp.float32)]
        + [pltpu.VMEM(block, jnp.bfloat16)] * (count - 1),
        compiler_params=PARAMS,
    )(slot, *in_hbm(x))
    return out[0], out[1:]


def value_kernel(count, slot_ref, rms_ref, own_ref, *refs):
    received, out_ref, kept_refs = refs[: count - 1], refs[count - 1], refs[count:-1]
    copies = started(received, kept_refs, refs[-1])
    slot = slot_ref[0]
    total = own_ref[...].astype(jnp.float32)
    for m in range(1, count):
        total += jnp.where(slot ^ m > slot, received[m - 1][...].astype(jnp.float32), 0.0)
    out_ref[...] = (total * rms_ref[:, :1]).astype(jnp.bfloat16)
    for copy in copies:
        copy.wait()


def value_grad(slot, inv_rms, own_term, received):
    block = own_term.shape
    count = len(received) + 1
    out = pl.pallas_call(
        functools.partial(value_kernel, count),
        in_specs=[SCALAR] + [IN_VMEM] * (count + 1),
        out_specs=[IN_VMEM] + [IN_HBM] * (count - 1),
        out_shape=[pltpu.VMEM(block, jnp.bfloat16)]
        + [pltpu.HBM(block, jnp.bfloat16)] * (count - 1),
        scratch_shapes=[pltpu.SemaphoreType.DMA((count - 1,))],
        compiler_params=PARAMS,
    )(slot, inv_rms, own_term, *received)
    return out[0], out[1:]


def hold_kernel(*refs):
    count = len(refs) // 2
    for in_ref, out_ref in zip(refs[:count], refs[count:]):
        out_ref[...] = in_ref[...]


def held(*arrays):
    rows, width = arrays[0].shape
    step = min(rows, 2 * TILE)
    wide = [pl.BlockSpec((step, width), lambda r: (r, 0))] * len(arrays)
    return pl.pallas_call(
        hold_kernel,
        grid=(rows // step,),
        in_specs=wide,
        out_specs=wide,
        out_shape=[pltpu.HBM(array.shape, array.dtype) for array in arrays],
        compiler_params=PARAMS,
    )(*arrays)


def column_kernel(count, slot_ref, gain_ref, own_ref, *refs):
    first, second, out_ref = refs[: count - 1], refs[count - 1 : -1], refs[-1]
    slot = slot_ref[0]
    rows = own_ref.shape[0]
    gain = gain_ref[...].astype(jnp.float32)
    for m in range(count):
        x = own_ref[...]
        if m > 0:
            x = jnp.where(slot ^ m > slot, first[m - 1][...], second[m - 1][...])
        out_ref[:, m * rows : (m + 1) * rows] = (x.astype(jnp.float32) * gain).astype(jnp.bfloat16).T


def gained_columns(slot, gain, x, first, second):
    count = len(first) + 1
    rows, width = x.shape
    width = width // count
    step = min(width, 256)
    steps = width // step
    column = pl.BlockSpec((rows, step), lambda c, _: (0, c))
    return pl.pallas_call(
        functools.partial(column_kernel, count),
        grid_spec=pltpu.PrefetchScalarGridSpec(
            num_scalar_prefetch=1,
            grid=(steps,),
            in_specs=[
                pl.BlockSpec((1, step), lambda c, _: (0, c)),
                pl.BlockSpec((rows, step), lambda c, slot_ref: (0, slot_ref[0] * steps + c)),
            ]
            + [column] * (2 * count - 2),
            out_specs=pl.BlockSpec((step, count * rows), lambda c, _: (c, 0)),
        ),
        out_shape=pltpu.VMEM((width, count * rows), jnp.bfloat16),
        compiler_params=PARAMS,
    )(slot, *in_hbm(gain, x), *first, *second)


def feature_kernel(count, weight_ref, gain_ref, *refs):
    value_refs, scaled_refs = refs[:count], refs[count:]
    rows = value_refs[0].shape[0]
    values = jnp.concatenate([ref[...] for ref in value_refs], axis=0)
    normed_grad = lax.dot_general(
        values, weight_ref[...], (((1,), (1,)), ((), ())), preferred_element_type=jnp.float32
    )
    gain = gain_ref[...].astype(jnp.float32)
    for m in range(count):
        scaled_refs[m][...] = (normed_grad[m * rows : (m + 1) * rows] * gain).astype(jnp.bfloat16)


def feature_grads(weight, gain, values):
    count = len(values)
    block = (values[0].shape[0], weight.shape[0])
    return pl.pallas_call(
        functools.partial(feature_kernel, count),
        in_specs=[IN_VMEM] * (count + 2),
        out_specs=[IN_VMEM] * count,
        out_shape=[pltpu.VMEM(block, jnp.bfloat16)] * count,
        compiler_params=PARAMS,
    )(weight, gain, *values)


def weight_product(half, width, weight_ref, gain_ref, columns_ref, value_refs):
    values = jnp.concatenate([ref[...] for ref in value_refs], axis=0)
    start = pl.multiple_of(half * width, width)
    lines = pl.ds(start, width)
    grad = jnp.dot(columns_ref[lines, :], values, preferred_element_type=jnp.float32)
    terms = grad * weight_ref[lines, :].astype(jnp.float32)
    lanes = sum(terms[:, i : i + DH] for i in range(0, grad.shape[1], DH))
    line = jnp.sum(lanes.T, axis=0, keepdims=True) / gain_ref[:, lines].astype(jnp.float32)
    return grad, line


def sent_kernel(half_ref, weight_ref, gain_ref, columns_ref, *refs):
    out_ref = refs[-1]
    width, kv_width = out_ref.shape[0] - TILE, out_ref.shape[1]
    grad, line = weight_product(half_ref[0], width, weight_ref, gain_ref, columns_ref, refs[:-1])
    out_ref[:width, :] = grad.astype(jnp.bfloat16)
    out_ref[width:, :] = jnp.zeros((TILE, kv_width), jnp.bfloat16)
    out_ref[width:, :width] = jnp.broadcast_to(line, (TILE, width)).astype(jnp.bfloat16)


def kept_kernel(half_ref, weight_ref, gain_ref, columns_ref, got_ref, *refs):
    out_ref, line_ref = refs[-2:]
    width = out_ref.shape[0]
    grad, line = weight_product(half_ref[0], width, weight_ref, gain_ref, columns_ref, refs[:-2])
    out_ref[...] = (grad + got_ref[:width, :].astype(jnp.float32)).astype(jnp.bfloat16)
    line_ref[...] = line + got_ref[width:, :width].astype(jnp.float32)[:1]


def weight_grad(half, halves, weight, gain, columns, values, got=None):
    kv_width = values[0].shape[1]
    width = columns.shape[0] // halves
    message = (width + TILE, kv_width)
    if got is None:
        kernel, extra = sent_kernel, []
        out_specs, out_shape = IN_VMEM, pltpu.VMEM(message, jnp.bfloat16)
    else:
        kernel, extra = kept_kernel, [got]
        out_specs = [fixed((width, kv_width)), fixed((1, width))]
        out_shape = [
            jax.ShapeDtypeStruct((width, kv_width), jnp.bfloat16),
            jax.ShapeDtypeStruct((1, width), jnp.float32),
        ]
    return pl.pallas_call(
        kernel,
        grid=(1,),
        in_specs=[SCALAR] + [IN_VMEM] * (3 + len(extra) + len(values)),
        out_specs=out_specs,
        out_shape=out_shape,
        compiler_params=PARAMS,
    )(half, weight, gain, columns, *extra, *values)


def stage_kernel(in_ref, out_ref):
    pltpu.sync_copy(in_ref, out_ref)


def staged(array):
    return pl.pallas_call(
        stage_kernel,
        in_specs=[IN_HBM],
        out_specs=IN_VMEM,
        out_shape=pltpu.VMEM(array.shape, array.dtype),
        compiler_params=PARAMS,
    )(*in_hbm(array))


def input_kernel(count, step, order, slot_ref, x_ref, grad_ref, *refs):
    scaled_refs, out_ref = refs[:count], refs[count]
    scaled_refs = [scaled_refs[order.index(m)] for m in range(count)]
    slot = slot_ref[0]
    lines = pl.ds(pl.multiple_of(pl.program_id(0) * step, step), step)
    x = x_ref[lines, :].astype(jnp.float32)
    square = 1.0 / (jnp.mean(x * x, axis=1, keepdims=True) + EPSILON)
    width = x.shape[1] // count
    places = [pl.ds(pl.multiple_of((slot ^ m) * width, width), width) for m in range(count)]
    inner = jnp.zeros_like(square)
    for m in range(count):
        block = x_ref[lines, places[m]].astype(jnp.float32)
        scaled = scaled_refs[m][lines, :].astype(jnp.float32)
        inner += jnp.sum(scaled * block, axis=1, keepdims=True)
    inner = inner * square / x.shape[1]
    for m in range(count):
        block = x_ref[lines, places[m]].astype(jnp.float32)
        grad = grad_ref[lines, places[m]].astype(jnp.float32)
        scaled = scaled_refs[m][lines, :].astype(jnp.float32)
        out_ref[:, places[m]] = (grad + (scaled - block * inner)).astype(jnp.bfloat16)


def input_grad(slot, x, grads, scaled, order):
    count = len(scaled)
    rows, width = x.shape
    step = min(rows, 4 * TILE)
    return pl.pallas_call(
        functools.partial(input_kernel, count, step, order),
        grid=(rows // step,),
        in_specs=[SCALAR] + [IN_VMEM] * (2 + count),
        out_specs=pl.BlockSpec((step, width), lambda r: (r, 0)),
        out_shape=jax.ShapeDtypeStruct((rows, width), jnp.bfloat16),
        compiler_params=PARAMS,
    )(slot, x, grads, *[scaled[m] for m in order])


def per_device(section_inputs, queries, keys, w_value, gain, section_grads_in):
    count = lax.axis_size("fsdp")
    docs = lax.axis_size("dp")
    slot = lax.axis_index("fsdp").astype(jnp.int32)[None]
    half = lax.axis_index("dp").astype(jnp.int32)[None]
    x, cotangent, own_keys = section_inputs[0, 0], section_grads_in[0, 0], keys[0, 0]
    weight = w_value[0]
    assert MEM <= x.shape[0] and docs == 2 and count & (count - 1) == 0
    masks = range(1, count)
    middle_first, far_first = [*masks[1:2], 1, *masks[2:]], masks[::-1]

    swap = [(0, 1), (1, 0)]

    sent_first = first_blocks(slot, own_keys, x, count)
    first = [to_partner(sent_first[m - 1], m) for m in masks]
    next_x = lax.ppermute(x, "section", section_route(-1))
    next_grad = lax.ppermute(cotangent, "section", section_route(-1))
    inv_rms, x_blocks = prepared(slot, x, count)
    query, grad, held_keys = staged(queries[0, 0]), staged(cotangent), staged(own_keys)
    first, inv_rms, x_blocks, query, grad, held_keys = after(
        (first, inv_rms, x_blocks, query, grad, held_keys), ()
    )
    terms, first = attention(slot, query, grad, [held_keys] + first, x_blocks)

    second = [to_partner(terms[m], m) for m in reversed(masks)][::-1]
    next_x, next_grad = held(next_x, next_grad)
    second, next_x, next_grad = after(([second[m - 1] for m in middle_first], next_x, next_grad), ())
    second = [second[middle_first.index(m)] for m in masks]
    value, second = value_grad(slot, inv_rms, terms[0], second)

    values = [value] + [to_partner(value, m) for m in masks]
    columns = gained_columns(slot, gain, x, first, second)
    weight, held_gain = staged(weight), staged(gain)
    others, columns, weight, held_gain = after(
        ([values[m] for m in far_first], columns, weight, held_gain), ()
    )
    values = [value] + [others[far_first.index(m)] for m in masks]

    sent = weight_grad(1 - half, docs, weight, held_gain, columns, values)
    scaled = feature_grads(weight, held_gain, values)
    returned = [to_partner(scaled[m], m, below=True) for m in range(count)]
    got = lax.ppermute(sent, "dp", swap)
    weight_out, gain_out = weight_grad(half, docs, weight, held_gain, columns, values, got)
    slot = after(slot, weight_out)
    passed = input_grad(slot, next_x, next_grad, returned, [*middle_first, 0])
    return passed[None, None], weight_out[None], gain_out


def solution(mesh):
    return jax.shard_map(
        per_device,
        mesh=mesh,
        in_specs=(
            P("section", "dp", "fsdp", None),
            P("section", "dp", "fsdp", None),
            P("section", "dp", "fsdp", None),
            P("section", "fsdp", None),
            P("section", "fsdp"),
            P("section", "dp", "fsdp", None),
        ),
        out_specs=(
            P("section", "dp", "fsdp", None),
            P("section", ("fsdp", "dp"), None),
            P("section", ("fsdp", "dp")),
        ),
        check_vma=False,
    )
```

```python
import functools

import jax
import jax.numpy as jnp
from jax import lax
from jax.experimental import pallas as pl
from jax.experimental.pallas import tpu as pltpu
from jax.sharding import PartitionSpec as P

DH = 128
MEM = 128
NEG_FILL = -1e30
EPSILON = 1e-05
LOG2E = 1.4426950408889634
TILE = 16
MIB = 1024 * 1024

SCALAR = pl.BlockSpec(memory_space=pltpu.SMEM)
IN_VMEM = pl.BlockSpec(memory_space=pltpu.VMEM)
IN_HBM = pl.BlockSpec(memory_space=pltpu.HBM)
PARAMS = pltpu.CompilerParams(vmem_limit_bytes=16 * MIB)


def section_route(distance):
    count = lax.axis_size("section")
    return [(s, (s + distance) % count) for s in range(count)]


def to_partner(block, mask, below=False):
    sections, count = lax.axis_size("section"), lax.axis_size("fsdp")
    route = [
        (s * count + f, (s - below) % sections * count + (f ^ mask))
        for s in range(sections)
        for f in range(count)
    ]
    return lax.ppermute(block, ("section", "fsdp"), route)


def after(arrays, others):
    kept, _ = lax.optimization_barrier((arrays, others))
    return kept


def fixed(shape):
    return pl.BlockSpec(shape, lambda *_: (0, 0))


def in_hbm(*arrays):
    return [pltpu.with_memory_space_constraint(array, pltpu.HBM) for array in arrays]


def started(refs, others, sems):
    copies = [
        pltpu.make_async_copy(ref, other, sems.at[i])
        for i, (ref, other) in enumerate(zip(refs, others))
    ]
    for copy in copies:
        copy.start()
    return copies


def attention_kernel(count, group, heads, slot_ref, query_ref, grad_ref, *refs):
    key_refs, x_refs = refs[:count], refs[count : 2 * count - 1]
    out_refs, kept_refs = refs[2 * count - 1 : 3 * count - 1], refs[3 * count - 1 : -1]
    copies = started(key_refs[1:], kept_refs, refs[-1])
    rows, kv_width = key_refs[0].shape
    slot = slot_ref[0]
    key_at = lax.broadcasted_iota(jnp.int32, (rows, rows), 0)
    query_at = lax.broadcasted_iota(jnp.int32, (rows, rows), 1)
    visible = (key_at <= query_at) | (slot * rows + key_at < MEM)
    visible = jnp.concatenate([visible] * group, axis=1)
    scale = DH ** (-0.5) * LOG2E

    def head_values(head, masks, hidden):
        own = pl.ds(pl.multiple_of(head * DH, DH), DH)
        members = [
            pl.ds(pl.multiple_of((head * group + h) * DH, DH), DH) for h in range(group)
        ]
        query = jnp.concatenate([query_ref[:, h] for h in members], axis=0)
        grad = jnp.concatenate([grad_ref[:, h] for h in members], axis=0)
        keys = jnp.concatenate([key_refs[m][:, own] for m in masks], axis=0)
        scores = lax.dot_general(
            keys, query, (((1,), (1,)), ((), ())), preferred_element_type=jnp.float32
        )
        parts = [scores[i * rows : (i + 1) * rows] for i in range(len(masks))]
        parts[0] = jnp.where(visible, parts[0], NEG_FILL)
        tops = [jnp.max(part, axis=0, keepdims=True) + hide for part, hide in zip(parts, hidden)]
        top = functools.reduce(jnp.maximum, tops)
        weights = [jnp.exp2((part - (top - hide)) * scale) for part, hide in zip(parts, hidden)]
        sums = [jnp.sum(weight, axis=0, keepdims=True) for weight in weights]
        inverse = 1.0 / functools.reduce(jnp.add, sums)
        probs = jnp.concatenate([(w * inverse).astype(jnp.bfloat16) for w in weights], axis=0)
        values = jnp.dot(probs, grad, preferred_element_type=jnp.float32)
        for i, m in enumerate(masks):
            out_refs[m][:, own] = values[i * rows : (i + 1) * rows].astype(jnp.bfloat16)

    def all_heads(masks, hidden):
        @pl.loop(0, kv_width // DH // heads)
        def _(step):
            for head in range(heads):
                head_values(step * heads + head, masks, hidden)

    if count <= 4:
        for place in range(count):
            masks = [0] + [m for m in range(1, count) if place ^ m < place]

            @pl.when(slot == place)
            def _():
                all_heads(masks, [0.0] * len(masks))

    else:
        hidden = [0.0] + [jnp.where(slot ^ m < slot, 0.0, NEG_FILL) for m in range(1, count)]
        all_heads(list(range(count)), hidden)

    for m in range(1, count):

        @pl.when(slot ^ m > slot)
        def _():
            out_refs[m][:, : x_refs[m - 1].shape[1]] = x_refs[m - 1][...]

    for copy in copies:
        copy.wait()


def attention(slot, queries, grads, key_blocks, x_blocks):
    rows, kv_width = key_blocks[0].shape
    group = queries.shape[1] // kv_width
    count = len(key_blocks)
    heads = min(8, kv_width // DH) if count <= 4 else 1
    assert x_blocks[0].shape[1] <= kv_width
    block = (rows, kv_width)
    out = pl.pallas_call(
        functools.partial(attention_kernel, count, group, heads),
        in_specs=[SCALAR] + [IN_VMEM] * (2 * count + 1),
        out_specs=[IN_VMEM] * count + [IN_HBM] * (count - 1),
        out_shape=[pltpu.VMEM(block, jnp.bfloat16)] * count
        + [pltpu.HBM(block, jnp.bfloat16)] * (count - 1),
        scratch_shapes=[pltpu.SemaphoreType.DMA((count - 1,))],
        compiler_params=pltpu.CompilerParams(vmem_limit_bytes=(12 + 2 * count) * MIB),
    )(slot, queries, grads, *key_blocks, *x_blocks)
    return out[:count], out[count:]


def first_kernel(count, slot_ref, keys_ref, x_ref, *refs):
    out_refs, sems = refs[:-1], refs[-1]
    slot = slot_ref[0]
    width = x_ref.shape[1] // count
    for m in range(1, count):
        out_ref = out_refs[m - 1]
        columns = pl.ds(pl.multiple_of((slot ^ m) * width, width), width)

        @pl.when(slot ^ m > slot)
        def _():
            pltpu.make_async_copy(keys_ref, out_ref, sems.at[m - 1]).start()

        @pl.when(slot ^ m < slot)
        def _():
            if width < out_ref.shape[1]:
                out_ref[:, width:] = jnp.zeros_like(out_ref[:, width:])
            pltpu.make_async_copy(
                x_ref.at[:, columns], out_ref.at[:, :width], sems.at[m - 1]
            ).start()

    for m in range(1, count):
        out_ref = out_refs[m - 1]

        @pl.when(slot ^ m > slot)
        def _():
            pltpu.make_async_copy(keys_ref, out_ref, sems.at[m - 1]).wait()

        @pl.when(slot ^ m < slot)
        def _():
            pltpu.make_async_copy(
                x_ref.at[:, :width], out_ref.at[:, :width], sems.at[m - 1]
            ).wait()


def first_blocks(slot, keys, x, count):
    return pl.pallas_call(
        functools.partial(first_kernel, count),
        in_specs=[SCALAR, IN_HBM, IN_HBM],
        out_specs=[IN_VMEM] * (count - 1),
        out_shape=[pltpu.VMEM(keys.shape, keys.dtype)] * (count - 1),
        scratch_shapes=[pltpu.SemaphoreType.DMA((count - 1,))],
        compiler_params=PARAMS,
    )(slot, *in_hbm(keys, x))


def prepare_kernel(count, slot_ref, x_ref, rms_ref, *out_refs):
    x = x_ref[...].astype(jnp.float32)
    inv_rms = lax.rsqrt(jnp.mean(x * x, axis=1, keepdims=True) + EPSILON)
    rms_ref[...] = jnp.broadcast_to(inv_rms, rms_ref.shape)
    width = x.shape[1] // count
    for m in range(1, count):
        start = pl.multiple_of((slot_ref[0] ^ m) * width, width)
        out_refs[m - 1][...] = x_ref[:, pl.ds(start, width)]


def prepared(slot, x, count):
    rows, width = x.shape
    step = min(rows, 2 * TILE)
    block = (rows, width // count)
    out = pl.pallas_call(
        functools.partial(prepare_kernel, count),
        grid=(rows // step,),
        in_specs=[SCALAR, pl.BlockSpec((step, width), lambda r: (r, 0))],
        out_specs=[pl.BlockSpec((step, DH), lambda r: (r, 0))]
        + [pl.BlockSpec((step, width // count), lambda r: (r, 0))] * (count - 1),
        out_shape=[pltpu.VMEM((rows, DH), jnp.float32)]
        + [pltpu.VMEM(block, jnp.bfloat16)] * (count - 1),
        compiler_params=PARAMS,
    )(slot, *in_hbm(x))
    return out[0], out[1:]


def value_kernel(count, slot_ref, rms_ref, own_ref, *refs):
    received, out_ref, kept_refs = refs[: count - 1], refs[count - 1], refs[count:-1]
    copies = started(received, kept_refs, refs[-1])
    slot = slot_ref[0]
    total = own_ref[...].astype(jnp.float32)
    for m in range(1, count):
        total += jnp.where(slot ^ m > slot, received[m - 1][...].astype(jnp.float32), 0.0)
    out_ref[...] = (total * rms_ref[:, :1]).astype(jnp.bfloat16)
    for copy in copies:
        copy.wait()


def value_grad(slot, inv_rms, own_term, received):
    block = own_term.shape
    count = len(received) + 1
    out = pl.pallas_call(
        functools.partial(value_kernel, count),
        in_specs=[SCALAR] + [IN_VMEM] * (count + 1),
        out_specs=[IN_VMEM] + [IN_HBM] * (count - 1),
        out_shape=[pltpu.VMEM(block, jnp.bfloat16)]
        + [pltpu.HBM(block, jnp.bfloat16)] * (count - 1),
        scratch_shapes=[pltpu.SemaphoreType.DMA((count - 1,))],
        compiler_params=PARAMS,
    )(slot, inv_rms, own_term, *received)
    return out[0], out[1:]


def hold_kernel(x_ref, grad_ref, x_out, grad_out, square_ref):
    x_out[...] = x_ref[...]
    grad_out[...] = grad_ref[...]
    x = x_ref[...].astype(jnp.float32)
    square = 1.0 / (jnp.mean(x * x, axis=1, keepdims=True) + EPSILON)
    square_ref[...] = jnp.broadcast_to(square, square_ref.shape)


def held(x, grads):
    rows, width = x.shape
    step = min(rows, 2 * TILE)
    wide = pl.BlockSpec((step, width), lambda r: (r, 0))
    return pl.pallas_call(
        hold_kernel,
        grid=(rows // step,),
        in_specs=[wide, wide],
        out_specs=[wide, wide, pl.BlockSpec((step, DH), lambda r: (r, 0))],
        out_shape=[pltpu.HBM(x.shape, x.dtype), pltpu.HBM(grads.shape, grads.dtype)]
        + [pltpu.HBM((rows, DH), jnp.float32)],
        compiler_params=PARAMS,
    )(x, grads)


def column_kernel(count, slot_ref, gain_ref, own_ref, *refs):
    first, second, out_ref = refs[: count - 1], refs[count - 1 : -1], refs[-1]
    slot = slot_ref[0]
    rows = own_ref.shape[0]
    gain = gain_ref[...].astype(jnp.float32)
    for m in range(count):
        x = own_ref[...]
        if m > 0:
            x = jnp.where(slot ^ m > slot, first[m - 1][...], second[m - 1][...])
        out_ref[:, m * rows : (m + 1) * rows] = (x.astype(jnp.float32) * gain).astype(jnp.bfloat16).T


def gained_columns(slot, gain, x, first, second):
    count = len(first) + 1
    rows, width = x.shape
    width = width // count
    step = min(width, 256)
    steps = width // step
    column = pl.BlockSpec((rows, step), lambda c, _: (0, c))
    return pl.pallas_call(
        functools.partial(column_kernel, count),
        grid_spec=pltpu.PrefetchScalarGridSpec(
            num_scalar_prefetch=1,
            grid=(steps,),
            in_specs=[
                pl.BlockSpec((1, step), lambda c, _: (0, c)),
                pl.BlockSpec((rows, step), lambda c, slot_ref: (0, slot_ref[0] * steps + c)),
            ]
            + [column] * (2 * count - 2),
            out_specs=pl.BlockSpec((step, count * rows), lambda c, _: (c, 0)),
        ),
        out_shape=pltpu.VMEM((width, count * rows), jnp.bfloat16),
        compiler_params=PARAMS,
    )(slot, *in_hbm(gain, x), *first, *second)


def feature_kernel(count, weight_ref, gain_ref, *refs):
    value_refs, scaled_refs = refs[:count], refs[count:]
    rows = value_refs[0].shape[0]
    values = jnp.concatenate([ref[...] for ref in value_refs], axis=0)
    normed_grad = lax.dot_general(
        values, weight_ref[...], (((1,), (1,)), ((), ())), preferred_element_type=jnp.float32
    )
    gain = gain_ref[...].astype(jnp.float32)
    for m in range(count):
        scaled_refs[m][...] = (normed_grad[m * rows : (m + 1) * rows] * gain).astype(jnp.bfloat16)


def feature_grads(weight, gain, values):
    count = len(values)
    block = (values[0].shape[0], weight.shape[0])
    return pl.pallas_call(
        functools.partial(feature_kernel, count),
        in_specs=[IN_VMEM] * (count + 2),
        out_specs=[IN_VMEM] * count,
        out_shape=[pltpu.VMEM(block, jnp.bfloat16)] * count,
        compiler_params=PARAMS,
    )(weight, gain, *values)


def weight_product(half, width, weight_ref, gain_ref, columns_ref, value_refs):
    values = jnp.concatenate([ref[...] for ref in value_refs], axis=0)
    start = pl.multiple_of(half * width, width)
    lines = pl.ds(start, width)
    grad = jnp.dot(columns_ref[lines, :], values, preferred_element_type=jnp.float32)
    terms = grad * weight_ref[lines, :].astype(jnp.float32)
    lanes = sum(terms[:, i : i + DH] for i in range(0, grad.shape[1], DH))
    line = jnp.sum(lanes.T, axis=0, keepdims=True) / gain_ref[:, lines].astype(jnp.float32)
    return grad, line


def sent_kernel(half_ref, weight_ref, gain_ref, columns_ref, *refs):
    out_ref = refs[-1]
    width, kv_width = out_ref.shape[0] - TILE, out_ref.shape[1]
    grad, line = weight_product(half_ref[0], width, weight_ref, gain_ref, columns_ref, refs[:-1])
    out_ref[:width, :] = grad.astype(jnp.bfloat16)
    out_ref[width:, :] = jnp.zeros((TILE, kv_width), jnp.bfloat16)
    out_ref[width:, :width] = jnp.broadcast_to(line, (TILE, width)).astype(jnp.bfloat16)


def kept_kernel(half_ref, weight_ref, gain_ref, columns_ref, got_ref, *refs):
    out_ref, line_ref = refs[-2:]
    width = out_ref.shape[0]
    grad, line = weight_product(half_ref[0], width, weight_ref, gain_ref, columns_ref, refs[:-2])
    out_ref[...] = (grad + got_ref[:width, :].astype(jnp.float32)).astype(jnp.bfloat16)
    line_ref[...] = line + got_ref[width:, :width].astype(jnp.float32)[:1]


def weight_grad(half, halves, weight, gain, columns, values, got=None):
    kv_width = values[0].shape[1]
    width = columns.shape[0] // halves
    message = (width + TILE, kv_width)
    if got is None:
        kernel, extra = sent_kernel, []
        out_specs, out_shape = IN_VMEM, pltpu.VMEM(message, jnp.bfloat16)
    else:
        kernel, extra = kept_kernel, [got]
        out_specs = [fixed((width, kv_width)), fixed((1, width))]
        out_shape = [
            jax.ShapeDtypeStruct((width, kv_width), jnp.bfloat16),
            jax.ShapeDtypeStruct((1, width), jnp.float32),
        ]
    return pl.pallas_call(
        kernel,
        grid=(1,),
        in_specs=[SCALAR] + [IN_VMEM] * (3 + len(extra) + len(values)),
        out_specs=out_specs,
        out_shape=out_shape,
        compiler_params=PARAMS,
    )(half, weight, gain, columns, *extra, *values)


def stage_kernel(in_ref, out_ref):
    pltpu.sync_copy(in_ref, out_ref)


def staged(array):
    return pl.pallas_call(
        stage_kernel,
        in_specs=[IN_HBM],
        out_specs=IN_VMEM,
        out_shape=pltpu.VMEM(array.shape, array.dtype),
        compiler_params=PARAMS,
    )(*in_hbm(array))


def input_kernel(count, step, order, slot_ref, x_ref, grad_ref, square_ref, *refs):
    scaled_refs, out_ref = refs[:count], refs[count]
    scaled_refs = [scaled_refs[order.index(m)] for m in range(count)]
    slot = slot_ref[0]
    lines = pl.ds(pl.multiple_of(pl.program_id(0) * step, step), step)
    square = square_ref[lines, :][:, :1]
    width = x_ref.shape[1] // count
    places = [pl.ds(pl.multiple_of((slot ^ m) * width, width), width) for m in range(count)]
    inner = jnp.zeros_like(square)
    for m in range(count):
        block = x_ref[lines, places[m]].astype(jnp.float32)
        scaled = scaled_refs[m][lines, :].astype(jnp.float32)
        inner += jnp.sum(scaled * block, axis=1, keepdims=True)
    inner = inner * square / x_ref.shape[1]
    for m in range(count):
        block = x_ref[lines, places[m]].astype(jnp.float32)
        grad = grad_ref[lines, places[m]].astype(jnp.float32)
        scaled = scaled_refs[m][lines, :].astype(jnp.float32)
        out_ref[:, places[m]] = (grad + (scaled - block * inner)).astype(jnp.bfloat16)


def input_grad(slot, x, grads, square, scaled, order):
    count = len(scaled)
    rows, width = x.shape
    step = min(rows, 4 * TILE)
    return pl.pallas_call(
        functools.partial(input_kernel, count, step, order),
        grid=(rows // step,),
        in_specs=[SCALAR] + [IN_VMEM] * (3 + count),
        out_specs=pl.BlockSpec((step, width), lambda r: (r, 0)),
        out_shape=jax.ShapeDtypeStruct((rows, width), jnp.bfloat16),
        compiler_params=PARAMS,
    )(slot, x, grads, square, *[scaled[m] for m in order])


def per_device(section_inputs, queries, keys, w_value, gain, section_grads_in):
    count = lax.axis_size("fsdp")
    docs = lax.axis_size("dp")
    slot = lax.axis_index("fsdp").astype(jnp.int32)[None]
    half = lax.axis_index("dp").astype(jnp.int32)[None]
    x, cotangent, own_keys = section_inputs[0, 0], section_grads_in[0, 0], keys[0, 0]
    weight = w_value[0]
    assert MEM <= x.shape[0] and docs == 2 and count & (count - 1) == 0
    masks = range(1, count)
    middle_first, far_first = [*masks[1:2], 1, *masks[2:]], masks[::-1]

    swap = [(0, 1), (1, 0)]

    sent_first = first_blocks(slot, own_keys, x, count)
    first = [to_partner(sent_first[m - 1], m) for m in masks]
    next_x = lax.ppermute(x, "section", section_route(-1))
    next_grad = lax.ppermute(cotangent, "section", section_route(-1))
    inv_rms, x_blocks = prepared(slot, x, count)
    query, grad, held_keys = staged(queries[0, 0]), staged(cotangent), staged(own_keys)
    first, inv_rms, x_blocks, query, grad, held_keys = after(
        (first, inv_rms, x_blocks, query, grad, held_keys), ()
    )
    terms, first = attention(slot, query, grad, [held_keys] + first, x_blocks)

    second = [to_partner(terms[m], m) for m in reversed(masks)][::-1]
    next_x, next_grad, square = held(next_x, next_grad)
    second, next_x, next_grad, square = after(
        ([second[m - 1] for m in middle_first], next_x, next_grad, square), ()
    )
    second = [second[middle_first.index(m)] for m in masks]
    value, second = value_grad(slot, inv_rms, terms[0], second)

    values = [value] + [to_partner(value, m) for m in masks]
    columns = gained_columns(slot, gain, x, first, second)
    weight, held_gain = staged(weight), staged(gain)
    others, columns, weight, held_gain = after(
        ([values[m] for m in far_first], columns, weight, held_gain), ()
    )
    values = [value] + [others[far_first.index(m)] for m in masks]

    sent = weight_grad(1 - half, docs, weight, held_gain, columns, values)
    scaled = feature_grads(weight, held_gain, values)
    returned = [to_partner(scaled[m], m, below=True) for m in range(count)]
    got = lax.ppermute(sent, "dp", swap)
    weight_out, gain_out = weight_grad(half, docs, weight, held_gain, columns, values, got)
    slot = after(slot, weight_out)
    passed = input_grad(slot, next_x, next_grad, square, returned, [*middle_first, 0])
    return passed[None, None], weight_out[None], gain_out


def solution(mesh):
    return jax.shard_map(
        per_device,
        mesh=mesh,
        in_specs=(
            P("section", "dp", "fsdp", None),
            P("section", "dp", "fsdp", None),
            P("section", "dp", "fsdp", None),
            P("section", "fsdp", None),
            P("section", "fsdp"),
            P("section", "dp", "fsdp", None),
        ),
        out_specs=(
            P("section", "dp", "fsdp", None),
            P("section", ("fsdp", "dp"), None),
            P("section", ("fsdp", "dp")),
        ),
        check_vma=False,
    )
```

```python
import functools

import jax
import jax.numpy as jnp
from jax import lax
from jax.experimental import pallas as pl
from jax.experimental.pallas import tpu as pltpu
from jax.sharding import PartitionSpec as P

DH = 128
MEM = 128
NEG_FILL = -1e30
EPSILON = 1e-05
LOG2E = 1.4426950408889634
TILE = 16
MIB = 1024 * 1024

SCALAR = pl.BlockSpec(memory_space=pltpu.SMEM)
IN_VMEM = pl.BlockSpec(memory_space=pltpu.VMEM)
IN_HBM = pl.BlockSpec(memory_space=pltpu.HBM)
PARAMS = pltpu.CompilerParams(vmem_limit_bytes=16 * MIB)


def section_route(distance):
    count = lax.axis_size("section")
    return [(s, (s + distance) % count) for s in range(count)]


def to_partner(block, mask, below=False):
    sections, count = lax.axis_size("section"), lax.axis_size("fsdp")
    route = [
        (s * count + f, (s - below) % sections * count + (f ^ mask))
        for s in range(sections)
        for f in range(count)
    ]
    return lax.ppermute(block, ("section", "fsdp"), route)


def after(arrays, others):
    kept, _ = lax.optimization_barrier((arrays, others))
    return kept


def fixed(shape):
    return pl.BlockSpec(shape, lambda *_: (0, 0))


def in_hbm(*arrays):
    return [pltpu.with_memory_space_constraint(array, pltpu.HBM) for array in arrays]


def started(refs, others, sems):
    copies = [
        pltpu.make_async_copy(ref, other, sems.at[i])
        for i, (ref, other) in enumerate(zip(refs, others))
    ]
    for copy in copies:
        copy.start()
    return copies


def attention_kernel(count, group, heads, slot_ref, query_ref, grad_ref, *refs):
    key_refs, x_refs = refs[:count], refs[count : 2 * count - 1]
    out_refs, kept_refs = refs[2 * count - 1 : 3 * count - 1], refs[3 * count - 1 : -1]
    copies = started(key_refs[1:], kept_refs, refs[-1])
    rows, kv_width = key_refs[0].shape
    slot = slot_ref[0]
    key_at = lax.broadcasted_iota(jnp.int32, (rows, rows), 0)
    query_at = lax.broadcasted_iota(jnp.int32, (rows, rows), 1)
    visible = (key_at <= query_at) | (slot * rows + key_at < MEM)
    visible = jnp.concatenate([visible] * group, axis=1)
    scale = DH ** (-0.5) * LOG2E

    def head_values(head, masks, hidden):
        own = pl.ds(pl.multiple_of(head * DH, DH), DH)
        members = [
            pl.ds(pl.multiple_of((head * group + h) * DH, DH), DH) for h in range(group)
        ]
        query = jnp.concatenate([query_ref[:, h] for h in members], axis=0)
        grad = jnp.concatenate([grad_ref[:, h] for h in members], axis=0)
        keys = jnp.concatenate([key_refs[m][:, own] for m in masks], axis=0)
        scores = lax.dot_general(
            keys, query, (((1,), (1,)), ((), ())), preferred_element_type=jnp.float32
        )
        parts = [scores[i * rows : (i + 1) * rows] for i in range(len(masks))]
        parts[0] = jnp.where(visible, parts[0], NEG_FILL)
        tops = [jnp.max(part, axis=0, keepdims=True) + hide for part, hide in zip(parts, hidden)]
        top = functools.reduce(jnp.maximum, tops)
        weights = [jnp.exp2((part - (top - hide)) * scale) for part, hide in zip(parts, hidden)]
        sums = [jnp.sum(weight, axis=0, keepdims=True) for weight in weights]
        inverse = 1.0 / functools.reduce(jnp.add, sums)
        probs = jnp.concatenate([(w * inverse).astype(jnp.bfloat16) for w in weights], axis=0)
        values = jnp.dot(probs, grad, preferred_element_type=jnp.float32)
        for i, m in enumerate(masks):
            out_refs[m][:, own] = values[i * rows : (i + 1) * rows].astype(jnp.bfloat16)

    def all_heads(masks, hidden):
        @pl.loop(0, kv_width // DH // heads)
        def _(step):
            for head in range(heads):
                head_values(step * heads + head, masks, hidden)

    if count <= 4:
        for place in range(count):
            masks = [0] + [m for m in range(1, count) if place ^ m < place]

            @pl.when(slot == place)
            def _():
                all_heads(masks, [0.0] * len(masks))

    else:
        hidden = [0.0] + [jnp.where(slot ^ m < slot, 0.0, NEG_FILL) for m in range(1, count)]
        all_heads(list(range(count)), hidden)

    for m in range(1, count):

        @pl.when(slot ^ m > slot)
        def _():
            out_refs[m][:, : x_refs[m - 1].shape[1]] = x_refs[m - 1][...]

    for copy in copies:
        copy.wait()


def attention(slot, queries, grads, key_blocks, x_blocks):
    rows, kv_width = key_blocks[0].shape
    group = queries.shape[1] // kv_width
    count = len(key_blocks)
    heads = min(8, kv_width // DH) if count <= 4 else 1
    assert x_blocks[0].shape[1] <= kv_width
    block = (rows, kv_width)
    out = pl.pallas_call(
        functools.partial(attention_kernel, count, group, heads),
        in_specs=[SCALAR] + [IN_VMEM] * (2 * count + 1),
        out_specs=[IN_VMEM] * count + [IN_HBM] * (count - 1),
        out_shape=[pltpu.VMEM(block, jnp.bfloat16)] * count
        + [pltpu.HBM(block, jnp.bfloat16)] * (count - 1),
        scratch_shapes=[pltpu.SemaphoreType.DMA((count - 1,))],
        compiler_params=pltpu.CompilerParams(vmem_limit_bytes=(12 + 2 * count) * MIB),
    )(slot, queries, grads, *key_blocks, *x_blocks)
    return out[:count], out[count:]


def first_kernel(count, slot_ref, keys_ref, x_ref, *refs):
    out_refs, sems = refs[:-1], refs[-1]
    slot = slot_ref[0]
    width = x_ref.shape[1] // count
    for m in range(1, count):
        out_ref = out_refs[m - 1]
        columns = pl.ds(pl.multiple_of((slot ^ m) * width, width), width)

        @pl.when(slot ^ m > slot)
        def _():
            pltpu.make_async_copy(keys_ref, out_ref, sems.at[m - 1]).start()

        @pl.when(slot ^ m < slot)
        def _():
            if width < out_ref.shape[1]:
                out_ref[:, width:] = jnp.zeros_like(out_ref[:, width:])
            pltpu.make_async_copy(
                x_ref.at[:, columns], out_ref.at[:, :width], sems.at[m - 1]
            ).start()

    for m in range(1, count):
        out_ref = out_refs[m - 1]

        @pl.when(slot ^ m > slot)
        def _():
            pltpu.make_async_copy(keys_ref, out_ref, sems.at[m - 1]).wait()

        @pl.when(slot ^ m < slot)
        def _():
            pltpu.make_async_copy(
                x_ref.at[:, :width], out_ref.at[:, :width], sems.at[m - 1]
            ).wait()


def first_blocks(slot, keys, x, count):
    return pl.pallas_call(
        functools.partial(first_kernel, count),
        in_specs=[SCALAR, IN_HBM, IN_HBM],
        out_specs=[IN_VMEM] * (count - 1),
        out_shape=[pltpu.VMEM(keys.shape, keys.dtype)] * (count - 1),
        scratch_shapes=[pltpu.SemaphoreType.DMA((count - 1,))],
        compiler_params=PARAMS,
    )(slot, *in_hbm(keys, x))


def prepare_kernel(count, slot_ref, x_ref, rms_ref, *out_refs):
    x = x_ref[...].astype(jnp.float32)
    inv_rms = lax.rsqrt(jnp.mean(x * x, axis=1, keepdims=True) + EPSILON)
    rms_ref[...] = jnp.broadcast_to(inv_rms, rms_ref.shape)
    width = x.shape[1] // count
    for m in range(1, count):
        start = pl.multiple_of((slot_ref[0] ^ m) * width, width)
        out_refs[m - 1][...] = x_ref[:, pl.ds(start, width)]


def prepared(slot, x, count):
    rows, width = x.shape
    step = min(rows, 2 * TILE)
    block = (rows, width // count)
    out = pl.pallas_call(
        functools.partial(prepare_kernel, count),
        grid=(rows // step,),
        in_specs=[SCALAR, pl.BlockSpec((step, width), lambda r: (r, 0))],
        out_specs=[pl.BlockSpec((step, DH), lambda r: (r, 0))]
        + [pl.BlockSpec((step, width // count), lambda r: (r, 0))] * (count - 1),
        out_shape=[pltpu.VMEM((rows, DH), jnp.float32)]
        + [pltpu.VMEM(block, jnp.bfloat16)] * (count - 1),
        compiler_params=PARAMS,
    )(slot, *in_hbm(x))
    return out[0], out[1:]


def value_kernel(count, slot_ref, rms_ref, own_ref, *refs):
    received, out_ref, kept_refs = refs[: count - 1], refs[count - 1], refs[count:-1]
    copies = started(received, kept_refs, refs[-1])
    slot = slot_ref[0]
    total = own_ref[...].astype(jnp.float32)
    for m in range(1, count):
        total += jnp.where(slot ^ m > slot, received[m - 1][...].astype(jnp.float32), 0.0)
    out_ref[...] = (total * rms_ref[:, :1]).astype(jnp.bfloat16)
    for copy in copies:
        copy.wait()


def value_grad(slot, inv_rms, own_term, received):
    block = own_term.shape
    count = len(received) + 1
    out = pl.pallas_call(
        functools.partial(value_kernel, count),
        in_specs=[SCALAR] + [IN_VMEM] * (count + 1),
        out_specs=[IN_VMEM] + [IN_HBM] * (count - 1),
        out_shape=[pltpu.VMEM(block, jnp.bfloat16)]
        + [pltpu.HBM(block, jnp.bfloat16)] * (count - 1),
        scratch_shapes=[pltpu.SemaphoreType.DMA((count - 1,))],
        compiler_params=PARAMS,
    )(slot, inv_rms, own_term, *received)
    return out[0], out[1:]


def hold_kernel(x_ref, grad_ref, x_out, grad_out, square_ref):
    x_out[...] = x_ref[...]
    grad_out[...] = grad_ref[...]
    x = x_ref[...].astype(jnp.float32)
    square = 1.0 / (jnp.mean(x * x, axis=1, keepdims=True) + EPSILON)
    square_ref[...] = jnp.broadcast_to(square, square_ref.shape)


def held(x, grads):
    rows, width = x.shape
    step = min(rows, 2 * TILE)
    wide = pl.BlockSpec((step, width), lambda r: (r, 0))
    return pl.pallas_call(
        hold_kernel,
        grid=(rows // step,),
        in_specs=[wide, wide],
        out_specs=[wide, wide, pl.BlockSpec((step, DH), lambda r: (r, 0))],
        out_shape=[pltpu.HBM(x.shape, x.dtype), pltpu.HBM(grads.shape, grads.dtype)]
        + [pltpu.HBM((rows, DH), jnp.float32)],
        compiler_params=PARAMS,
    )(x, grads)


def column_kernel(count, slot_ref, gain_ref, own_ref, *refs):
    first, second, out_ref = refs[: count - 1], refs[count - 1 : -1], refs[-1]
    slot = slot_ref[0]
    rows = own_ref.shape[0]
    gain = gain_ref[...].astype(jnp.float32)
    for m in range(count):
        x = own_ref[...]
        if m > 0:
            x = jnp.where(slot ^ m > slot, first[m - 1][...], second[m - 1][...])
        out_ref[:, m * rows : (m + 1) * rows] = (x.astype(jnp.float32) * gain).astype(jnp.bfloat16).T


def gained_columns(slot, gain, x, first, second):
    count = len(first) + 1
    rows, width = x.shape
    width = width // count
    step = min(width, 256)
    steps = width // step
    column = pl.BlockSpec((rows, step), lambda c, _: (0, c))
    return pl.pallas_call(
        functools.partial(column_kernel, count),
        grid_spec=pltpu.PrefetchScalarGridSpec(
            num_scalar_prefetch=1,
            grid=(steps,),
            in_specs=[
                pl.BlockSpec((1, step), lambda c, _: (0, c)),
                pl.BlockSpec((rows, step), lambda c, slot_ref: (0, slot_ref[0] * steps + c)),
            ]
            + [column] * (2 * count - 2),
            out_specs=pl.BlockSpec((step, count * rows), lambda c, _: (c, 0)),
        ),
        out_shape=pltpu.VMEM((width, count * rows), jnp.bfloat16),
        compiler_params=PARAMS,
    )(slot, *in_hbm(gain, x), *first, *second)


def feature_kernel(count, weight_ref, gain_ref, *refs):
    value_refs, scaled_refs = refs[:count], refs[count:]
    rows = value_refs[0].shape[0]
    values = jnp.concatenate([ref[...] for ref in value_refs], axis=0)
    normed_grad = lax.dot_general(
        values, weight_ref[...], (((1,), (1,)), ((), ())), preferred_element_type=jnp.float32
    )
    gain = gain_ref[...].astype(jnp.float32)
    for m in range(count):
        scaled_refs[m][...] = (normed_grad[m * rows : (m + 1) * rows] * gain).astype(jnp.bfloat16)


def feature_grads(weight, gain, values):
    count = len(values)
    block = (values[0].shape[0], weight.shape[0])
    return pl.pallas_call(
        functools.partial(feature_kernel, count),
        in_specs=[IN_VMEM] * (count + 2),
        out_specs=[IN_VMEM] * count,
        out_shape=[pltpu.VMEM(block, jnp.bfloat16)] * count,
        compiler_params=PARAMS,
    )(weight, gain, *values)


def weight_product(half, width, weight_ref, gain_ref, columns_ref, value_refs):
    values = jnp.concatenate([ref[...] for ref in value_refs], axis=0)
    start = pl.multiple_of(half * width, width)
    lines = pl.ds(start, width)
    grad = jnp.dot(columns_ref[lines, :], values, preferred_element_type=jnp.float32)
    terms = grad * weight_ref[lines, :].astype(jnp.float32)
    lanes = sum(terms[:, i : i + DH] for i in range(0, grad.shape[1], DH))
    line = jnp.sum(lanes.T, axis=0, keepdims=True) / gain_ref[:, lines].astype(jnp.float32)
    return grad, line


def sent_kernel(half_ref, weight_ref, gain_ref, columns_ref, *refs):
    out_ref = refs[-1]
    width, kv_width = out_ref.shape[0] - TILE, out_ref.shape[1]
    grad, line = weight_product(half_ref[0], width, weight_ref, gain_ref, columns_ref, refs[:-1])
    out_ref[:width, :] = grad.astype(jnp.bfloat16)
    out_ref[width:, :] = jnp.zeros((TILE, kv_width), jnp.bfloat16)
    out_ref[width:, :width] = jnp.broadcast_to(line, (TILE, width)).astype(jnp.bfloat16)


def kept_kernel(half_ref, weight_ref, gain_ref, columns_ref, got_ref, *refs):
    out_ref, line_ref = refs[-2:]
    width = out_ref.shape[0]
    grad, line = weight_product(half_ref[0], width, weight_ref, gain_ref, columns_ref, refs[:-2])
    out_ref[...] = (grad + got_ref[:width, :].astype(jnp.float32)).astype(jnp.bfloat16)
    line_ref[...] = line + got_ref[width:, :width].astype(jnp.float32)[:1]


def weight_grad(half, halves, weight, gain, columns, values, got=None):
    kv_width = values[0].shape[1]
    width = columns.shape[0] // halves
    message = (width + TILE, kv_width)
    if got is None:
        kernel, extra = sent_kernel, []
        out_specs, out_shape = IN_VMEM, pltpu.VMEM(message, jnp.bfloat16)
    else:
        kernel, extra = kept_kernel, [got]
        out_specs = [fixed((width, kv_width)), fixed((1, width))]
        out_shape = [
            jax.ShapeDtypeStruct((width, kv_width), jnp.bfloat16),
            jax.ShapeDtypeStruct((1, width), jnp.float32),
        ]
    return pl.pallas_call(
        kernel,
        grid=(1,),
        in_specs=[SCALAR] + [IN_VMEM] * (3 + len(extra) + len(values)),
        out_specs=out_specs,
        out_shape=out_shape,
        compiler_params=PARAMS,
    )(half, weight, gain, columns, *extra, *values)


def turn_kernel(count, half_ref, weight_ref, gain_ref, columns_ref, *refs):
    value_refs, out_refs = refs[:count], refs[count:]
    feature_kernel(count, weight_ref, gain_ref, *value_refs, *out_refs[:count])
    sent_kernel(half_ref, weight_ref, gain_ref, columns_ref, *value_refs, out_refs[count])


def turned(half, halves, weight, gain, columns, values):
    count = len(values)
    rows, kv_width = values[0].shape
    width = weight.shape[0]
    message = (width // halves + TILE, kv_width)
    out = pl.pallas_call(
        functools.partial(turn_kernel, count),
        in_specs=[SCALAR] + [IN_VMEM] * (count + 3),
        out_specs=[IN_VMEM] * (count + 1),
        out_shape=[pltpu.VMEM((rows, width), jnp.bfloat16)] * count
        + [pltpu.VMEM(message, jnp.bfloat16)],
        compiler_params=PARAMS,
    )(half, weight, gain, columns, *values)
    return out[:count], out[count]


def stage_kernel(in_ref, out_ref):
    pltpu.sync_copy(in_ref, out_ref)


def staged(array):
    return pl.pallas_call(
        stage_kernel,
        in_specs=[IN_HBM],
        out_specs=IN_VMEM,
        out_shape=pltpu.VMEM(array.shape, array.dtype),
        compiler_params=PARAMS,
    )(*in_hbm(array))


def input_kernel(count, step, order, slot_ref, x_ref, grad_ref, square_ref, *refs):
    scaled_refs, out_ref = refs[:count], refs[count]
    scaled_refs = [scaled_refs[order.index(m)] for m in range(count)]
    slot = slot_ref[0]
    lines = pl.ds(pl.multiple_of(pl.program_id(0) * step, step), step)
    square = square_ref[lines, :][:, :1]
    width = x_ref.shape[1] // count
    places = [pl.ds(pl.multiple_of((slot ^ m) * width, width), width) for m in range(count)]
    inner = jnp.zeros_like(square)
    for m in range(count):
        block = x_ref[lines, places[m]].astype(jnp.float32)
        scaled = scaled_refs[m][lines, :].astype(jnp.float32)
        inner += jnp.sum(scaled * block, axis=1, keepdims=True)
    inner = inner * square / x_ref.shape[1]
    for m in range(count):
        block = x_ref[lines, places[m]].astype(jnp.float32)
        grad = grad_ref[lines, places[m]].astype(jnp.float32)
        scaled = scaled_refs[m][lines, :].astype(jnp.float32)
        out_ref[:, places[m]] = (grad + (scaled - block * inner)).astype(jnp.bfloat16)


def input_grad(slot, x, grads, square, scaled, order):
    count = len(scaled)
    rows, width = x.shape
    step = min(rows, 4 * TILE)
    return pl.pallas_call(
        functools.partial(input_kernel, count, step, order),
        grid=(rows // step,),
        in_specs=[SCALAR] + [IN_VMEM] * (3 + count),
        out_specs=pl.BlockSpec((step, width), lambda r: (r, 0)),
        out_shape=jax.ShapeDtypeStruct((rows, width), jnp.bfloat16),
        compiler_params=PARAMS,
    )(slot, x, grads, square, *[scaled[m] for m in order])


def per_device(section_inputs, queries, keys, w_value, gain, section_grads_in):
    count = lax.axis_size("fsdp")
    docs = lax.axis_size("dp")
    slot = lax.axis_index("fsdp").astype(jnp.int32)[None]
    half = lax.axis_index("dp").astype(jnp.int32)[None]
    x, cotangent, own_keys = section_inputs[0, 0], section_grads_in[0, 0], keys[0, 0]
    weight = w_value[0]
    assert MEM <= x.shape[0] and docs == 2 and count & (count - 1) == 0
    masks = range(1, count)
    middle_first, gather_order = [*masks[1:2], 1, *masks[2:]], list(masks)

    swap = [(0, 1), (1, 0)]

    sent_first = first_blocks(slot, own_keys, x, count)
    first = [to_partner(sent_first[m - 1], m) for m in masks]
    next_x = lax.ppermute(x, "section", section_route(-1))
    next_grad = lax.ppermute(cotangent, "section", section_route(-1))
    inv_rms, x_blocks = prepared(slot, x, count)
    query, grad, held_keys = staged(queries[0, 0]), staged(cotangent), staged(own_keys)
    first, inv_rms, x_blocks, query, grad, held_keys = after(
        (first, inv_rms, x_blocks, query, grad, held_keys), ()
    )
    terms, first = attention(slot, query, grad, [held_keys] + first, x_blocks)

    second = [to_partner(terms[m], m) for m in reversed(masks)][::-1]
    next_x, next_grad, square = held(next_x, next_grad)
    second, next_x, next_grad, square = after(
        ([second[m - 1] for m in middle_first], next_x, next_grad, square), ()
    )
    second = [second[middle_first.index(m)] for m in masks]
    value, second = value_grad(slot, inv_rms, terms[0], second)

    values = [value] + [to_partner(value, m) for m in masks]
    columns = gained_columns(slot, gain, x, first, second)
    weight, held_gain = staged(weight), staged(gain)
    others, columns, weight, held_gain = after(
        ([values[m] for m in gather_order], columns, weight, held_gain), ()
    )
    values = [value] + [others[gather_order.index(m)] for m in masks]

    scaled, sent = turned(1 - half, docs, weight, held_gain, columns, values)
    returned = [to_partner(scaled[m], m, below=True) for m in range(count)]
    got = lax.ppermute(sent, "dp", swap)
    weight_out, gain_out = weight_grad(half, docs, weight, held_gain, columns, values, got)
    slot = after(slot, weight_out)
    passed = input_grad(slot, next_x, next_grad, square, returned, [*middle_first, 0])
    return passed[None, None], weight_out[None], gain_out


def solution(mesh):
    return jax.shard_map(
        per_device,
        mesh=mesh,
        in_specs=(
            P("section", "dp", "fsdp", None),
            P("section", "dp", "fsdp", None),
            P("section", "dp", "fsdp", None),
            P("section", "fsdp", None),
            P("section", "fsdp"),
            P("section", "dp", "fsdp", None),
        ),
        out_specs=(
            P("section", "dp", "fsdp", None),
            P("section", ("fsdp", "dp"), None),
            P("section", ("fsdp", "dp")),
        ),
        check_vma=False,
    )
```
